512 devices in a mesh: panel: 2 (over y_lo), lat: 16 (over z), lon: 16 (over y_hi, x, core).
Axes of the slice: x: 4, y: 4 (y_hi: 2, y_lo: 2; y = y_hi * 2 + y_lo), z: 16, core: 2. Of those that a mesh axis runs over, the one named last changes fastest.
Arguments:
- state: float32 [2, 7, 2, 1024, 2048], P('panel', None, None, 'lat', 'lon'), may hold values from -4 to 4
- source_slot: int32 [2, 16, 16, 768], P('panel', 'lat', 'lon'), may hold values from 0 to 12287, as said below
- donor_cell: int32 [2, 16, 16, 48], P('panel', 'lat', 'lon'), may hold values from 0 to 8000
- donor_frac: float32 [2, 16, 16, 2, 48], P('panel', 'lat', 'lon'), may hold values from 0 to 1
- donor_turn: float32 [2, 16, 16, 48], P('panel', 'lat', 'lon'), may hold values from -3.140625 to 3.140625
Outputs:
- new_state: float32 [2, 7, 2, 1024, 2048], P('panel', None, None, 'lat', 'lon')
The draws below stay inside these ranges and needn't reach their ends.
Inputs may be any that keep to these rules, and one draw needn't show every extreme that they name: `source_slot`: entries name a partner panel donation (a * 16 + b) * 48 + s. For a device on an edge of its panel, the rim entries that lie on that edge name the donations that fill them; over a panel's whole border every donation of the partner panel is named exactly once. Other entries are unused.
All inputs are finite; a program needn't handle non-finite values.
Results may differ from the reference program's by a relative error of at most 0.00002.
Values sent between devices are 32-bit elements; how exact they have to be, the bound alone decides.
A program may use at most 64 MiB of HBM per device.

```python
import jax
import jax.numpy as jnp

COMPS = 7
NR = 2
CLAT = 64
CLON = 128
LAT = 1024
LON = 2048
DON = 48
N_PANEL = 2
N_LAT = 16
N_LON = 16


def draw_source_slot(key, part):
    total = 4 * (N_LAT * CLAT + N_LON * CLON)
    rim_len = 4 * (CLAT + CLON)
    band = 2 * CLON
    side = 2 * CLAT

    def one_panel(sub):
        key_order, key_fill = jax.random.split(sub)
        order = jax.random.permutation(key_order, total).astype(jnp.int32)
        filler = jax.random.randint(key_fill, (N_LAT, N_LON, rim_len), 0, total, dtype=jnp.int32)
        rows_a = jnp.arange(N_LAT, dtype=jnp.int32)[:, None, None]
        cols_b = jnp.arange(N_LON, dtype=jnp.int32)[None, :, None]
        place = jnp.arange(rim_len, dtype=jnp.int32)[None, None, :]
        on_top = (rows_a == 0) & (place < band)
        on_bottom = (rows_a == N_LAT - 1) & (place >= band) & (place < 2 * band)
        on_left = (cols_b == 0) & (place >= 2 * band) & (place < 2 * band + side)
        on_right = (cols_b == N_LON - 1) & (place >= 2 * band + side)
        k_top = cols_b * band + place
        k_bottom = N_LON * band + cols_b * band + (place - band)
        k_left = 2 * N_LON * band + rows_a * side + (place - 2 * band)
        k_right = 2 * N_LON * band + N_LAT * side + rows_a * side + (place - 2 * band - side)
        border = jnp.where(on_top, k_top, jnp.where(on_bottom, k_bottom, jnp.where(on_left, k_left, k_right)))
        on_edge = on_top | on_bottom | on_left | on_right
        picked = jnp.take(order, jnp.clip(border, 0, total - 1))
        return jnp.where(on_edge, picked, filler)
    return jnp.stack([one_panel(jax.random.fold_in(key, 11)), one_panel(jax.random.fold_in(key, 12))])


def plant(array, rng, smallest, top_value):
    longest = array.shape.index(max(array.shape))
    spots = []
    for shift in (0, 1):
        where = [jax.random.randint(jax.random.fold_in(rng, axis), (), 0, length) for axis, length in enumerate(array.shape)]
        where[longest] = (where[longest] + shift) % array.shape[longest]
        spots.append(tuple(where))
    return array.at[spots[0]].set(smallest).at[spots[1]].set(top_value)


def steps_of(rng, shape, cuts, low, high):
    loudness, own = 1.0, jax.random.fold_in(rng, 6)
    for position, blocks in cuts:
        steps = jnp.exp(jax.random.uniform(jax.random.fold_in(own, position), (blocks,), jnp.float32, low / len(cuts), high / len(cuts)))
        loudness = loudness * jnp.repeat(steps, shape[position] // blocks).reshape([-1 if axis == position else 1 for axis in range(len(shape))])
    return loudness


def bell_draw(stream_key, shape, scale, most, shards=(), held_as=jnp.bfloat16):
    result = jax.random.normal(stream_key, shape, jnp.float32) * scale
    if len(shards) > 0:
        result = steps_of(stream_key, shape, shards, -0.22, 0.18) * result
    return jnp.clip(result, min=-most, max=most).astype(held_as)


def setup_inputs(seed: int = 0) -> dict:
    key_of = jax.random.split(jax.random.key(seed), 6)
    state = bell_draw(key_of[0], (N_PANEL, COMPS, NR, LAT, LON), 1.0, 4.0, ((0, 2), (3, 16), (4, 16)), jnp.float32)
    source_slot = draw_source_slot(jax.random.fold_in(key_of[5], 71), 0)
    donor_cell = plant(jax.random.randint(key_of[2], (N_PANEL, N_LAT, N_LON, DON), 0, (CLAT - 1) * (CLON - 1)), jax.random.fold_in(key_of[2], 1), 0, ((CLAT - 1) * (CLON - 1)) - 1).astype(jnp.int32)
    donor_frac = jnp.clip(1.0 * jax.random.uniform(key_of[3], (N_PANEL, N_LAT, N_LON, 2, DON), jnp.float32) ** steps_of(key_of[3], (N_PANEL, N_LAT, N_LON, 2, DON), ((0, 2), (1, 16), (2, 16)), -0.2, 0.2), 0.0, 1.0)
    donor_turn = jnp.clip(jax.random.uniform(key_of[4], (N_PANEL, N_LAT, N_LON, DON), jnp.float32, -3.140625, 3.140625), -3.140625, 3.140625)
    return {"state": state, "source_slot": source_slot, "donor_cell": donor_cell, "donor_frac": donor_frac, "donor_turn": donor_turn}


viscosity = 0.05
resistivity = 0.05
diffusivity = 0.05
buoyancy = 0.5
time_step = 0.25


def rate(ext):
    height = ext.shape[2] - 4
    width = ext.shape[3] - 4

    def lat_at(k):
        return ext[:, :, 2 + k:2 + k + height, 2:2 + width]

    def lon_at(k):
        return ext[:, :, 2:2 + height, 2 + k:2 + k + width]

    middle = lat_at(0)
    d_lat = (8.0 * (lat_at(1) - lat_at(-1)) - (lat_at(2) - lat_at(-2))) / 12.0
    d_lon = (8.0 * (lon_at(1) - lon_at(-1)) - (lon_at(2) - lon_at(-2))) / 12.0
    padded = jnp.pad(middle, ((0, 0), (1, 1), (0, 0), (0, 0)))
    lap = lat_at(1) + lat_at(-1) + lon_at(1) + lon_at(-1) - 4.0 * middle
    lap = lap + padded[:, 2:] + padded[:, :-2] - 2.0 * middle
    adv_u = middle[1:2] * d_lat + middle[2:3] * d_lon
    adv_b = middle[4:5] * d_lat + middle[5:6] * d_lon
    moment = -adv_u[0:3] + adv_b[3:6] + viscosity * lap[0:3]
    induct = adv_b[0:3] - adv_u[3:6] + resistivity * lap[3:6]
    heat = -adv_u[6:7] + diffusivity * lap[6:7]
    first = moment[0:1] + buoyancy * middle[6:7]
    return jnp.concatenate([first, moment[1:3], induct, heat], axis=0)


def rotate(values, turn):
    cosine = jnp.cos(turn)
    sine = jnp.sin(turn)
    parts = [values[0],
             cosine * values[1] - sine * values[2],
             sine * values[1] + cosine * values[2],
             values[3],
             cosine * values[4] - sine * values[5],
             sine * values[4] + cosine * values[5],
             values[6]]
    return jnp.stack(parts)


def donate(field, donor_cell, donor_frac, donor_turn):
    lat_dev = donor_cell.shape[0]
    lon_dev = donor_cell.shape[1]
    rows_a = jnp.arange(lat_dev, dtype=jnp.int32)[:, None, None]
    cols_b = jnp.arange(lon_dev, dtype=jnp.int32)[None, :, None]
    row = rows_a * CLAT + donor_cell // (CLON - 1)
    col = cols_b * CLON + donor_cell % (CLON - 1)
    index = (row * LON + col).reshape(-1).astype(jnp.int32)
    flat = field.reshape(COMPS, NR, LAT * LON)
    lower = jnp.take(flat, index, axis=2)
    lower_next = jnp.take(flat, index + 1, axis=2)
    upper = jnp.take(flat, index + LON, axis=2)
    upper_next = jnp.take(flat, index + LON + 1, axis=2)
    frac_t = donor_frac[:, :, 0, :].reshape(-1)
    frac_p = donor_frac[:, :, 1, :].reshape(-1)
    value = ((1.0 - frac_t) * (1.0 - frac_p) * lower + (1.0 - frac_t) * frac_p * lower_next
             + frac_t * (1.0 - frac_p) * upper + frac_t * frac_p * upper_next)
    return rotate(value, donor_turn.reshape(-1))


def extend(field, donation, slots):
    lat_dev = slots.shape[0]
    lon_dev = slots.shape[1]
    rim_values = jnp.take(donation, slots, axis=2)
    ext = jnp.pad(field, ((0, 0), (0, 0), (2, 2), (2, 2)))
    top = rim_values[:, :, 0, :, 0:2 * CLON].reshape(COMPS, NR, lon_dev, 2, CLON)
    top = jnp.transpose(top, (0, 1, 3, 2, 4)).reshape(COMPS, NR, 2, LON)
    bottom = rim_values[:, :, lat_dev - 1, :, 2 * CLON:4 * CLON].reshape(COMPS, NR, lon_dev, 2, CLON)
    bottom = jnp.transpose(bottom, (0, 1, 3, 2, 4)).reshape(COMPS, NR, 2, LON)
    left = rim_values[:, :, :, 0, 4 * CLON:4 * CLON + 2 * CLAT].reshape(COMPS, NR, lat_dev, 2, CLAT)
    left = jnp.transpose(left, (0, 1, 2, 4, 3)).reshape(COMPS, NR, LAT, 2)
    right = rim_values[:, :, :, lon_dev - 1, 4 * CLON + 2 * CLAT:].reshape(COMPS, NR, lat_dev, 2, CLAT)
    right = jnp.transpose(right, (0, 1, 2, 4, 3)).reshape(COMPS, NR, LAT, 2)
    ext = ext.at[:, :, 0:2, 2:2 + LON].set(top)
    ext = ext.at[:, :, LAT + 2:LAT + 4, 2:2 + LON].set(bottom)
    ext = ext.at[:, :, 2:2 + LAT, 0:2].set(left)
    ext = ext.at[:, :, 2:2 + LAT, LON + 2:LON + 4].set(right)
    return ext


def section_rate(fields, source_slot, donor_cell, donor_frac, donor_turn):
    given = [donate(fields[q], donor_cell[q], donor_frac[q], donor_turn[q]) for q in range(2)]
    rates = [rate(extend(fields[p], given[1 - p], source_slot[p])) for p in range(2)]
    return jnp.stack(rates)


def reference(state, source_slot, donor_cell, donor_frac, donor_turn):
    section_one = state + time_step * section_rate(state, source_slot, donor_cell, donor_frac, donor_turn)
    second = section_rate(section_one, source_slot, donor_cell, donor_frac, donor_turn)
    return 0.5 * state + 0.5 * (section_one + time_step * second)
```

```python
import functools

import jax
import jax.numpy as jnp
from jax import lax
from jax.experimental import pallas as pl
from jax.experimental.pallas import tpu as pltpu
from jax.sharding import PartitionSpec as P

MESH = pl.DeviceIdType.MESH
DIFFUSION = 0.05
BUOYANCY = 0.5
STEP = 0.25
PAD = 8
UP, DOWN, LEFT, RIGHT = range(4)


def lane_take(value, index):
    return jnp.take_along_axis(value, index, axis=1, mode="promise_in_bounds")


def kernel(
    n_lat, n_lon, state, slots, cell, frac, turn, out,
    ext, whole_i, whole_f, pack, pack_from, don, gathered, idx, parts, top, bottom, left, right, flip,
    load_sem, send_a, recv_a, send_h, recv_h, send_i, recv_i, send_b, recv_b,
):
    comps, levels, rows, cols = state.shape[1:]
    n_slots = cell.shape[3]
    half = cols // 2
    side = 2 * rows
    q = lax.axis_index("panel")
    a = lax.axis_index("lat")
    b = lax.axis_index("lon")
    other = 1 - q
    first_a, last_a = a == 0, a == n_lat - 1
    first_b, last_b = b == 0, b == n_lon - 1

    neighbours = (
        (a > 0, (q, a - 1, b)),
        (a < n_lat - 1, (q, a + 1, b)),
        (b > 0, (q, a, b - 1)),
        (b < n_lon - 1, (q, a, b + 1)),
    )
    receivers = (
        (q, 0, b),
        (q, n_lat - 1, b),
        (q, b, 0),
        (q, b, n_lon - 1),
    )
    is_receiver = (first_a, last_a, first_b, last_b)
    own = (
        first_a,
        last_a,
        jnp.logical_and(first_a, first_b),
        jnp.logical_and(last_a, last_b),
    )

    def selector(role, k):
        return (q, k, b) if role < 2 else (q, k, a)

    def is_me(role, k):
        return (k == a) if role < 2 else jnp.logical_and(k == a, b == a)

    load = pltpu.make_async_copy(
        state.at[0], ext.at[0, :, :, pl.ds(PAD, rows), :], load_sem
    )
    load.start()

    barrier = pltpu.get_barrier_semaphore()

    def greet(device):
        pl.semaphore_signal(barrier, inc=1, device_id=device, device_id_type=MESH)

    @pl.loop(0, n_lon)
    def _(k):
        greet((other, a, k))

    for there, device in neighbours:
        pl.when(there)(functools.partial(greet, device))
    for role in range(4):
        pl.when(jnp.logical_not(own[role]))(functools.partial(greet, receivers[role]))

        @pl.when(is_receiver[role])
        def _():
            @pl.loop(0, n_lat)
            def _(k):
                pl.when(jnp.logical_not(is_me(role, k)))(
                    lambda: greet(selector(role, k))
                )

    whole_i[...] = jnp.zeros_like(whole_i)
    whole_f[...] = jnp.zeros_like(whole_f)
    for start in (0, half):
        whole_i[0:1, start : start + n_slots] = cell[0, 0]
        whole_f[0:1, start : start + n_slots] = turn[0, 0]
        whole_f[1:3, start : start + n_slots] = frac[0, 0, 0]
    cells = whole_i[0:1, :]
    turns = whole_f[0:1, :]
    cosine = jnp.cos(turns)
    sine = jnp.sin(turns)
    frac_t = whole_f[1:2, :]
    frac_p = whole_f[2:3, :]
    row = (cells * 33027) >> 22
    col = cells - row * (cols - 1)
    row_at = lax.broadcasted_iota(jnp.int32, (rows, cols), 0)
    row_full = jnp.broadcast_to(row, (rows, cols))
    weight_t = jnp.where(
        row_at == row_full,
        jnp.broadcast_to(1.0 - frac_t, (rows, cols)),
        jnp.where(row_at == row_full + 1, jnp.broadcast_to(frac_t, (rows, cols)), 0.0),
    )
    lane = lax.broadcasted_iota(jnp.int32, (rows, cols), 1)
    low_lane = lane < half
    lower_at = jnp.broadcast_to(col, (rows, cols))
    upper_at = lower_at + 1
    left_p = jnp.broadcast_to(1.0 - frac_p, (rows, cols))
    right_p = jnp.broadcast_to(frac_p, (rows, cols))
    lane8 = lax.broadcasted_iota(jnp.int32, (8, cols), 1)

    def inner(s, c, level, shift=0):
        return ext[s, c, level, PAD + shift : PAD + shift + rows, :]

    def donate(s):
        given = []
        for c in range(comps):
            low, high = inner(s, c, 0), inner(s, c, 1)
            one = jnp.where(low_lane, lane_take(low, lower_at), lane_take(high, lower_at))
            two = jnp.where(low_lane, lane_take(low, upper_at), lane_take(high, upper_at))
            mixed = (left_p * one + right_p * two) * weight_t
            given.append(jnp.sum(mixed, axis=0, keepdims=True))
        for i in (1, 4):
            x, y = given[i], given[i + 1]
            given[i], given[i + 1] = cosine * x - sine * y, sine * x + cosine * y
        for c in range(comps):
            don[s, c : c + 1, :] = given[c]
        don[s, comps : comps + 1, :] = jnp.zeros((1, cols), jnp.float32)

    def pack_sides(s):
        packed = jnp.zeros((rows, cols), jnp.float32)
        for f in range(comps * levels):
            turned = pltpu.roll(inner(s, f // levels, f % levels), 4 * f + 2, 1)
            packed = jnp.where(lane >> 2 == f, turned, packed)
        pack[s] = packed

    def halo_copies(s):
        e = ext.at[s]
        pairs = (
            (e.at[:, :, pl.ds(PAD, 8), :], e.at[:, :, pl.ds(PAD + rows, 8), :]),
            (e.at[:, :, pl.ds(PAD + rows - 8, 8), :], e.at[:, :, pl.ds(PAD - 8, 8), :]),
            (pack.at[s], pack_from.at[s, 1]),
            (pack.at[s], pack_from.at[s, 0]),
        )
        copies = []
        for to, (src, dst) in enumerate(pairs):
            copies.append(
                pltpu.make_async_remote_copy(
                    src_ref=src,
                    dst_ref=dst,
                    send_sem=send_h.at[s, to],
                    recv_sem=recv_h.at[s, to],
                    device_id=neighbours[to][1],
                    device_id_type=MESH,
                )
            )
        return copies

    def wait_bytes(ref, sem):
        pltpu.make_async_copy(ref, ref, sem).wait()

    def start_halo(s):
        for (there, _), copy in zip(neighbours, halo_copies(s)):
            pl.when(there)(copy.start)

    def start_a(s):
        @pl.loop(0, n_lon)
        def _(k):
            pltpu.make_async_remote_copy(
                src_ref=don.at[s],
                dst_ref=gathered.at[s, b],
                send_sem=send_a.at[s],
                recv_sem=recv_a.at[s],
                device_id=(other, a, k),
                device_id_type=MESH,
            ).start()

    ranges = ((0, 2 * cols), (2 * cols, 2 * cols), (4 * cols, side), (4 * cols + side, side))

    def index_copy(role, k):
        start, size = ranges[role]
        return pltpu.make_async_remote_copy(
            src_ref=slots.at[0, 0, :, pl.ds(start, size)],
            dst_ref=idx.at[:, pl.ds(start, size)],
            send_sem=send_i.at[role, k],
            recv_sem=recv_i.at[role],
            device_id=selector(role, k),
            device_id_type=MESH,
        )

    def each_selector(role, action):
        @pl.when(is_receiver[role])
        def _():
            @pl.loop(0, n_lat)
            def _(k):
                @pl.when(jnp.logical_not(is_me(role, k)))
                def _():
                    action(index_copy(role, k))

    buffers = (top, bottom, left, right)
    pieces = ((0, 2), (2, 2), (4, 1), (5, 1))

    def part_copy(s, role):
        start, size = pieces[role]
        return pltpu.make_async_remote_copy(
            src_ref=parts.at[s, pl.ds(start, size)],
            dst_ref=buffers[role].at[s, a],
            send_sem=send_b.at[s, role],
            recv_sem=recv_b.at[s, role],
            device_id=receivers[role],
            device_id_type=MESH,
        )

    def select(s):
        for tile in range(6):
            wanted = idx[0:1, tile * cols : (tile + 1) * cols] - a * (n_lon * n_slots)
            known = jnp.logical_and(wanted >= 0, wanted < n_lon * n_slots)
            wanted = jnp.where(known, wanted, 0)
            giver = ((wanted >> 4) * 21846) >> 16
            place = jnp.broadcast_to(wanted - giver * n_slots, (8, cols))
            giver = jnp.broadcast_to(jnp.where(known, giver, -1), (8, cols))

            def body(k, totals):
                block = gathered[s, k]
                mine = giver == k
                return tuple(
                    jnp.where(mine, lane_take(block, place + level * half), total)
                    for level, total in enumerate(totals)
                )

            zero = jnp.zeros((8, cols), jnp.float32)
            for level, total in enumerate(lax.fori_loop(0, n_lon, body, (zero, zero))):
                parts[s, tile, level] = total

    def start_b(s):
        for role in range(4):
            start, size = pieces[role]
            pl.when(jnp.logical_not(own[role]))(part_copy(s, role).start)

            @pl.when(own[role])
            def _():
                buffers[role][s, a] = parts[s, start : start + size]

    def take_rim(s):
        for role, buffer in enumerate(buffers):

            @pl.when(is_receiver[role])
            def _():
                if role % 2 == 0:
                    others = buffer.at[s, pl.ds(1, n_lat - 1)]
                else:
                    others = buffer.at[s, pl.ds(0, n_lat - 1)]
                sem = recv_b.at[s, role]
                if role < 2:
                    wait_bytes(others, sem)
                else:
                    pl.when(own[role])(lambda: wait_bytes(others, sem))
                    pl.when(jnp.logical_not(own[role]))(
                        lambda: wait_bytes(buffer.at[s], sem)
                    )
                total = jnp.sum(buffer[s], axis=0)
                if role < 2:
                    at = PAD - 2 if role == 0 else PAD + rows
                    for t in range(2):
                        for level in range(levels):
                            for c in range(comps):
                                ext[s, c, level, at + t : at + t + 1, :] = total[
                                    t, level, c : c + 1, :
                                ]
                else:
                    flip[...] = jnp.zeros_like(flip)
                    for level in range(levels):
                        both = (total[0, level], pltpu.roll(total[0, level], half, 1))
                        for t in range(2):
                            for c in range(comps):
                                at = 4 * (c * levels + level) + 2 * (role - 2) + t
                                flip[at : at + 1, :] = both[t][c : c + 1, :]
                    pack_from[s, role - 2] = flip[...].T[0:rows, :]

    def wait_halo(s):
        landed = (
            ext.at[s, :, :, pl.ds(PAD - 8, 8), :],
            ext.at[s, :, :, pl.ds(PAD + rows, 8), :],
            pack_from.at[s, 0],
            pack_from.at[s, 1],
        )
        for side_of, opposite in ((UP, DOWN), (DOWN, UP), (LEFT, RIGHT), (RIGHT, LEFT)):
            ref, sem = landed[side_of], recv_h.at[s, opposite]
            pl.when(neighbours[side_of][0])(functools.partial(wait_bytes, ref, sem))

    def rates(s, emit, chunk):
        for base in range(0, rows, chunk):
            lanes = lane[0:chunk]
            edge = jnp.where(
                lanes & 2 == 0,
                pack_from[s, 0, base : base + chunk, :],
                pack_from[s, 1, base : base + chunk, :],
            )

            def at(c, level, shift=0):
                low = PAD + base + shift
                return ext[s, c, level, low : low + chunk, :]

            for level in range(levels):
                u1, u2 = at(1, level) * (1.0 / 12.0), at(2, level) * (1.0 / 12.0)
                b1, b2 = at(4, level) * (1.0 / 12.0), at(5, level) * (1.0 / 12.0)

                def terms(c, with_b):
                    mid = at(c, level)
                    around = pltpu.roll(edge, (cols - 2 - 4 * (c * levels + level)) % cols, 1)
                    west1 = pltpu.roll(jnp.where(lanes == cols - 1, around, mid), 1, 1)
                    west2 = pltpu.roll(jnp.where(lanes >= cols - 2, around, mid), 2, 1)
                    east1 = pltpu.roll(jnp.where(lanes == 0, around, mid), cols - 1, 1)
                    east2 = pltpu.roll(jnp.where(lanes < 2, around, mid), cols - 2, 1)
                    north1, south1 = at(c, level, -1), at(c, level, 1)
                    d_lat = 8.0 * (south1 - north1) - (at(c, level, 2) - at(c, level, -2))
                    d_lon = 8.0 * (east1 - west1) - (east2 - west2)
                    lap = south1 + north1 + east1 + west1 + at(c, 1 - level) - 6.0 * mid
                    adv_u = u1 * d_lat + u2 * d_lon
                    adv_b = b1 * d_lat + b2 * d_lon if with_b else None
                    return mid, adv_u, adv_b, DIFFUSION * lap

                for c in range(3):
                    mid, adv_u, adv_b, lap = terms(c, True)
                    mid_b, adv_ub, adv_bb, lap_b = terms(c + 3, True)
                    moment = adv_bb - adv_u + lap
                    if c == 0:
                        moment = moment + BUOYANCY * at(6, level)
                    emit(c, level, base, mid, moment)
                    emit(c + 3, level, base, mid_b, adv_b - adv_ub + lap_b)
                mid, adv_u, _, lap = terms(6, False)
                emit(6, level, base, mid, lap - adv_u)

    chunk = 32

    def first_section(c, level, base, mid, rate):
        ext[1, c, level, PAD + base : PAD + base + chunk, :] = mid + STEP * rate

    def second_section(c, level, base, mid, rate):
        start = ext[0, c, level, PAD + base : PAD + base + chunk, :]
        out[0, c, level, base : base + chunk, :] = 0.5 * start + 0.5 * (mid + STEP * rate)

    load.wait()
    donate(0)
    pack_sides(0)

    count = n_lon
    for there, _ in neighbours:
        count = count + there.astype(jnp.int32)
    for role in range(4):
        count = count + jnp.logical_not(own[role]).astype(jnp.int32)
        count = count + jnp.where(
            is_receiver[role], n_lat - own[role].astype(jnp.int32), 0
        )
    pl.semaphore_wait(barrier, count)

    for s in range(2):
        if s == 1:
            donate(1)
            pack_sides(1)
        start_a(s)
        if s == 0:
            for role in range(4):
                each_selector(role, lambda copy: copy.start())
        start_halo(s)
        if s == 0:
            for role in range(4):
                start, size = ranges[role]
                here = idx.at[:, pl.ds(start, size)]

                @pl.when(own[role])
                def _():
                    idx[:, start : start + size] = slots[0, 0, :, start : start + size]

                pl.when(jnp.logical_not(own[role]))(
                    functools.partial(wait_bytes, here, recv_i.at[role])
                )
        wait_bytes(gathered.at[s], recv_a.at[s])
        select(s)
        start_b(s)
        wait_halo(s)
        take_rim(s)
        rates(s, first_section if s == 0 else second_section, chunk)

    for s in range(2):
        wait_bytes(gathered.at[s], send_a.at[s])
        for (there, _), copy in zip(neighbours, halo_copies(s)):
            pl.when(there)(copy.wait_send)
        for role in range(4):
            pl.when(jnp.logical_not(own[role]))(part_copy(s, role).wait_send)
    for role in range(4):
        each_selector(role, lambda copy: copy.wait_send())


def solution(mesh):
    n_lat, n_lon = mesh.shape["lat"], mesh.shape["lon"]

    def per_device(state, source_slot, donor_cell, donor_frac, donor_turn):
        _, comps, levels, rows, cols = state.shape
        f32, i32, dma = jnp.float32, jnp.int32, pltpu.SemaphoreType.DMA
        vmem = pl.BlockSpec(memory_space=pltpu.VMEM)
        return pl.pallas_call(
            functools.partial(kernel, n_lat, n_lon),
            out_shape=jax.ShapeDtypeStruct(state.shape, f32),
            in_specs=[pl.BlockSpec(memory_space=pl.ANY)] + [vmem] * 4,
            out_specs=vmem,
            scratch_shapes=[
                pltpu.VMEM((2, comps, levels, rows + 2 * PAD, cols), f32),
                pltpu.VMEM((8, cols), i32),
                pltpu.VMEM((8, cols), f32),
                pltpu.VMEM((2, rows, cols), f32),
                pltpu.VMEM((2, 2, rows, cols), f32),
                pltpu.VMEM((2, 8, cols), f32),
                pltpu.VMEM((2, n_lon, 8, cols), f32),
                pltpu.VMEM((1, 4 * cols + 4 * rows), i32),
                pltpu.VMEM((2, 6, levels, 8, cols), f32),
                pltpu.VMEM((2, n_lat, 2, levels, 8, cols), f32),
                pltpu.VMEM((2, n_lat, 2, levels, 8, cols), f32),
                pltpu.VMEM((2, n_lat, 1, levels, 8, cols), f32),
                pltpu.VMEM((2, n_lat, 1, levels, 8, cols), f32),
                pltpu.VMEM((cols, cols), f32),
                dma,
                dma((2,)),
                dma((2,)),
                dma((2, 4)),
                dma((2, 4)),
                dma((4, n_lat)),
                dma((4,)),
                dma((2, 4)),
                dma((2, 4)),
            ],
            compiler_params=pltpu.CompilerParams(
                collective_id=0, has_side_effects=True, vmem_limit_bytes=32 * 2**20
            ),
        )(state, source_slot, donor_cell, donor_frac, donor_turn)

    in_specs = (
        P("panel", None, None, "lat", "lon"),
        P("panel", "lat", "lon", None),
        P("panel", "lat", "lon", None),
        P("panel", "lat", "lon", None, None),
        P("panel", "lat", "lon", None),
    )
    out_specs = P("panel", None, None, "lat", "lon")
    return jax.shard_map(
        per_device, mesh=mesh, in_specs=in_specs, out_specs=out_specs, check_vma=False
    )
```

```python
import functools

import jax
import jax.numpy as jnp
from jax import lax
from jax.experimental import pallas as pl
from jax.experimental.pallas import tpu as pltpu
from jax.sharding import PartitionSpec as P

MESH = pl.DeviceIdType.MESH
DIFFUSION = 0.05
BUOYANCY = 0.5
STEP = 0.25
PAD = 8
UP, DOWN, LEFT, RIGHT = range(4)


def lane_take(value, index):
    return jnp.take_along_axis(value, index, axis=1, mode="promise_in_bounds")


def kernel(
    n_lat, n_lon, state, slots, cell, frac, turn, out,
    ext, cell_at, turn_at, frac_at, whole_i, whole_f, pack, pack_from, gathered, idx_rows, idx_sides,
    row_parts, side_parts, row_rim, side_rim, flip,
    load_sem, send_a, recv_a, send_h, recv_h, send_i, recv_i, send_b, recv_b,
):
    comps, levels, rows, cols = state.shape[1:]
    n_slots = cell.shape[3]
    half = cols // 2
    p = lax.axis_index("panel")
    a = lax.axis_index("lat")
    b = lax.axis_index("lon")
    other = 1 - p
    first_a, last_a = a == 0, a == n_lat - 1
    first_b, last_b = b == 0, b == n_lon - 1
    edge_a = jnp.logical_or(first_a, last_a)
    edge_b = jnp.logical_or(first_b, last_b)
    edge = jnp.logical_or(edge_a, edge_b)

    neighbours = (
        (a > 0, (p, a - 1, b)),
        (a < n_lat - 1, (p, a + 1, b)),
        (b > 0, (p, a, b - 1)),
        (b < n_lon - 1, (p, a, b + 1)),
    )

    loads = [
        pltpu.make_async_copy(cell.at[0, 0], cell_at, load_sem.at[1]),
        pltpu.make_async_copy(turn.at[0, 0], turn_at, load_sem.at[2]),
        pltpu.make_async_copy(frac.at[0, 0, 0], frac_at, load_sem.at[3]),
        pltpu.make_async_copy(
            state.at[0], ext.at[0, :, :, pl.ds(PAD, rows), :], load_sem.at[0]
        ),
    ]
    for load in loads:
        load.start()

    barrier = pltpu.get_barrier_semaphore()

    def greet(device):
        pl.semaphore_signal(barrier, inc=1, device_id=device, device_id_type=MESH)

    @pl.loop(0, n_lon)
    def _(k):
        greet((other, a, k))

    @pl.loop(1, n_lat)
    def _(k):
        greet((p, lax.rem(a + k, n_lat), b))

    for there, device in neighbours[2:]:
        pl.when(there)(functools.partial(greet, device))
    greeted = n_lon + n_lat - 1 + (b > 0).astype(jnp.int32) + (b < n_lon - 1).astype(jnp.int32)

    for load in loads[:3]:
        load.wait()
    whole_i[...] = jnp.zeros_like(whole_i)
    whole_f[...] = jnp.zeros_like(whole_f)
    for start in (0, half):
        whole_i[0:1, start : start + n_slots] = cell_at[...]
        whole_f[0:1, start : start + n_slots] = turn_at[...]
        whole_f[1:3, start : start + n_slots] = frac_at[...]
    cells = whole_i[0:1, :]
    turns = whole_f[0:1, :]
    cosine = jnp.cos(turns)
    sine = jnp.sin(turns)
    frac_t = whole_f[1:2, :]
    frac_p = whole_f[2:3, :]
    row = (cells * 33027) >> 22
    col = cells - row * (cols - 1)
    row_at = lax.broadcasted_iota(jnp.int32, (rows, cols), 0)
    row_full = jnp.broadcast_to(row, (rows, cols))
    weight_t = jnp.where(
        row_at == row_full,
        jnp.broadcast_to(1.0 - frac_t, (rows, cols)),
        jnp.where(row_at == row_full + 1, jnp.broadcast_to(frac_t, (rows, cols)), 0.0),
    )
    lane = lax.broadcasted_iota(jnp.int32, (rows, cols), 1)
    low_lane = lane < half
    lower_at = jnp.broadcast_to(col, (rows, cols))
    upper_at = lower_at + 1
    left_p = jnp.broadcast_to(1.0 - frac_p, (rows, cols))
    right_p = jnp.broadcast_to(frac_p, (rows, cols))
    lane8 = lax.broadcasted_iota(jnp.int32, (8, cols), 1)

    def inner(s, c, level, shift=0):
        return ext[s, c, level, PAD + shift : PAD + shift + rows, :]

    def donate(s):
        given = []
        for c in range(comps):
            low, high = inner(s, c, 0), inner(s, c, 1)
            one = jnp.where(low_lane, lane_take(low, lower_at), lane_take(high, lower_at))
            two = jnp.where(low_lane, lane_take(low, upper_at), lane_take(high, upper_at))
            mixed = (left_p * one + right_p * two) * weight_t
            given.append(jnp.sum(mixed, axis=0, keepdims=True))
        for i in (1, 4):
            x, y = given[i], given[i + 1]
            given[i], given[i + 1] = cosine * x - sine * y, sine * x + cosine * y
        for c in range(comps):
            gathered[s, a, c : c + 1, :] = given[c]
        gathered[s, a, comps : comps + 1, :] = jnp.zeros((1, cols), jnp.float32)

    def pack_sides(s):
        packed = jnp.zeros((rows, cols), jnp.float32)
        for f in range(comps * levels):
            turned = pltpu.roll(inner(s, f // levels, f % levels), 4 * f + 2, 1)
            packed = jnp.where(lane >> 2 == f, turned, packed)
        pack[s] = packed

    def halo_copies(s):
        e = ext.at[s]
        pairs = (
            (e.at[:, :, pl.ds(PAD, 8), :], e.at[:, :, pl.ds(PAD + rows, 8), :]),
            (e.at[:, :, pl.ds(PAD + rows - 8, 8), :], e.at[:, :, pl.ds(PAD - 8, 8), :]),
            (pack.at[s], pack_from.at[s, 1]),
            (pack.at[s], pack_from.at[s, 0]),
        )
        copies = []
        for to, (src, dst) in enumerate(pairs):
            copies.append(
                pltpu.make_async_remote_copy(
                    src_ref=src,
                    dst_ref=dst,
                    send_sem=send_h.at[s, to],
                    recv_sem=recv_h.at[s, to],
                    device_id=neighbours[to][1],
                    device_id_type=MESH,
                )
            )
        return copies

    def wait_bytes(ref, sem):
        pltpu.make_async_copy(ref, ref, sem).wait()

    def start_halo(s):
        for (there, _), copy in zip(neighbours, halo_copies(s)):
            pl.when(there)(copy.start)

    def start_a(s):
        @pl.loop(1, n_lat)
        def _(k):
            pltpu.make_async_remote_copy(
                src_ref=gathered.at[s, a],
                dst_ref=gathered.at[s, a],
                send_sem=send_a.at[s],
                recv_sem=recv_a.at[s],
                device_id=(p, lax.rem(a + k, n_lat), b),
                device_id_type=MESH,
            ).start()

    def wait_a(s, sem):
        wait_bytes(gathered.at[s, pl.ds(0, n_lat - 1)], sem.at[s])

    def send_slots():
        def send(start, dst, kind):
            size = dst.shape[-1]

            @pl.loop(0, n_lon)
            def _(k):
                pltpu.make_async_remote_copy(
                    src_ref=slots.at[0, 0, :, pl.ds(start, size)],
                    dst_ref=dst,
                    send_sem=send_i.at[kind],
                    recv_sem=recv_i.at[kind],
                    device_id=(other, a, k),
                    device_id_type=MESH,
                ).start()

        pl.when(first_a)(lambda: send(0, idx_rows.at[b], 0))
        pl.when(last_a)(lambda: send(2 * cols, idx_rows.at[b], 0))
        pl.when(first_b)(lambda: send(4 * cols, idx_sides.at[0], 1))
        pl.when(last_b)(lambda: send(4 * cols + 2 * rows, idx_sides.at[1], 1))

    def wait_slots():
        pl.when(edge_a)(lambda: wait_bytes(idx_rows, recv_i.at[0]))
        wait_bytes(idx_sides, recv_i.at[1])

    def pick(s, wanted):
        device = ((wanted >> 4) * 21846) >> 16
        place = jnp.broadcast_to(wanted - device * n_slots, (8, cols))
        row_of = device >> (n_lon.bit_length() - 1)
        giver = jnp.where(device - row_of * n_lon == b, row_of, -1)
        giver = jnp.broadcast_to(giver, (8, cols))
        totals = [jnp.zeros((8, cols), jnp.float32)] * levels
        places = [place + level * half for level in range(levels)]
        for k in range(n_lat):
            block = gathered[s, k]
            mine = giver == k
            for level in range(levels):
                totals[level] = jnp.where(mine, lane_take(block, places[level]), totals[level])
        return totals

    def send_parts(s):
        def to(src, dst, kind, k):
            return pltpu.make_async_remote_copy(
                src_ref=src,
                dst_ref=dst.at[s, b],
                send_sem=send_b.at[s, kind],
                recv_sem=recv_b.at[s, kind],
                device_id=(other, a, k),
                device_id_type=MESH,
            )

        for side in range(2):
            for level, total in enumerate(pick(s, idx_sides[side])):
                side_parts[s, side, level] = total
            to(side_parts.at[s, side], side_rim, 1, side * (n_lon - 1)).start()

        @pl.when(edge_a)
        def _():
            @pl.loop(0, n_lon)
            def _(k):
                for t in range(2):
                    for level, total in enumerate(
                        pick(s, idx_rows[k, :, t * cols : (t + 1) * cols])
                    ):
                        row_parts[s, k, t, level] = total
                to(row_parts.at[s, k], row_rim, 0, k).start()

    def take_rim(s):
        @pl.when(edge_a)
        def _():
            wait_bytes(row_rim.at[s], recv_b.at[s, 0])
            total = jnp.sum(row_rim[s], axis=0)

            def put(at):
                for t in range(2):
                    for level in range(levels):
                        for c in range(comps):
                            ext[s, c, level, at + t : at + t + 1, :] = total[t, level, c : c + 1, :]

            pl.when(first_a)(lambda: put(PAD - 2))
            pl.when(last_a)(lambda: put(PAD + rows))

        @pl.when(edge_b)
        def _():
            wait_bytes(side_rim.at[s], recv_b.at[s, 1])
            total = jnp.sum(side_rim[s], axis=0)

            def put(side):
                flip[...] = jnp.zeros_like(flip)
                for level in range(levels):
                    both = (total[level], pltpu.roll(total[level], half, 1))
                    for t in range(2):
                        for c in range(comps):
                            at = 4 * (c * levels + level) + 2 * side + t
                            flip[at : at + 1, :] = both[t][c : c + 1, :]
                pack_from[s, side] = flip[...].T[0:rows, :]

            pl.when(first_b)(lambda: put(0))
            pl.when(last_b)(lambda: put(1))

    def wait_halo(s):
        landed = (
            ext.at[s, :, :, pl.ds(PAD - 8, 8), :],
            ext.at[s, :, :, pl.ds(PAD + rows, 8), :],
            pack_from.at[s, 0],
            pack_from.at[s, 1],
        )
        for side_of, opposite in ((UP, DOWN), (DOWN, UP), (LEFT, RIGHT), (RIGHT, LEFT)):
            ref, sem = landed[side_of], recv_h.at[s, opposite]
            pl.when(neighbours[side_of][0])(functools.partial(wait_bytes, ref, sem))

    def rates(s, emit, chunk):
        for base in range(0, rows, chunk):
            lanes = lane[0:chunk]
            beside = jnp.where(
                lanes & 2 == 0,
                pack_from[s, 0, base : base + chunk, :],
                pack_from[s, 1, base : base + chunk, :],
            )

            def at(c, level, shift=0):
                low = PAD + base + shift
                return ext[s, c, level, low : low + chunk, :]

            for level in range(levels):
                u1, u2 = at(1, level) * (1.0 / 12.0), at(2, level) * (1.0 / 12.0)
                b1, b2 = at(4, level) * (1.0 / 12.0), at(5, level) * (1.0 / 12.0)

                def terms(c, with_b):
                    mid = at(c, level)
                    around = pltpu.roll(beside, (cols - 2 - 4 * (c * levels + level)) % cols, 1)
                    west1 = pltpu.roll(jnp.where(lanes == cols - 1, around, mid), 1, 1)
                    west2 = pltpu.roll(jnp.where(lanes >= cols - 2, around, mid), 2, 1)
                    east1 = pltpu.roll(jnp.where(lanes == 0, around, mid), cols - 1, 1)
                    east2 = pltpu.roll(jnp.where(lanes < 2, around, mid), cols - 2, 1)
                    north1, south1 = at(c, level, -1), at(c, level, 1)
                    d_lat = 8.0 * (south1 - north1) - (at(c, level, 2) - at(c, level, -2))
                    d_lon = 8.0 * (east1 - west1) - (east2 - west2)
                    lap = south1 + north1 + east1 + west1 + at(c, 1 - level) - 6.0 * mid
                    adv_u = u1 * d_lat + u2 * d_lon
                    adv_b = b1 * d_lat + b2 * d_lon if with_b else None
                    return mid, adv_u, adv_b, DIFFUSION * lap

                for c in range(3):
                    mid, adv_u, adv_b, lap = terms(c, True)
                    mid_b, adv_ub, adv_bb, lap_b = terms(c + 3, True)
                    moment = adv_bb - adv_u + lap
                    if c == 0:
                        moment = moment + BUOYANCY * at(6, level)
                    emit(c, level, base, mid, moment)
                    emit(c + 3, level, base, mid_b, adv_b - adv_ub + lap_b)
                mid, adv_u, _, lap = terms(6, False)
                emit(6, level, base, mid, lap - adv_u)

    chunk = rows

    def first_section(c, level, base, mid, rate):
        ext[1, c, level, PAD + base : PAD + base + chunk, :] = mid + STEP * rate

    def second_section(c, level, base, mid, rate):
        start = ext[0, c, level, PAD + base : PAD + base + chunk, :]
        out[0, c, level, base : base + chunk, :] = 0.5 * start + 0.5 * (mid + STEP * rate)

    def give(s):
        donate(s)
        if s == 0:
            pl.semaphore_wait(barrier, greeted)
        start_a(s)
        if s == 0:
            send_slots()
        pack_sides(s)
        start_halo(s)

    def first_half():
        rates(0, first_section, chunk)
        give(1)

    loads[3].wait()
    give(0)
    wait_halo(0)
    pl.when(jnp.logical_not(edge))(first_half)
    wait_a(0, recv_a)
    wait_slots()
    send_parts(0)

    @pl.when(edge)
    def _():
        take_rim(0)
        first_half()

    wait_a(1, recv_a)
    send_parts(1)
    wait_halo(1)
    pl.when(edge)(lambda: take_rim(1))
    rates(1, second_section, chunk)

    for s in range(2):
        wait_a(s, send_a)
        for (there, _), copy in zip(neighbours, halo_copies(s)):
            pl.when(there)(copy.wait_send)
        wait_bytes(side_parts.at[s], send_b.at[s, 1])
        pl.when(edge_a)(functools.partial(wait_bytes, row_parts.at[s], send_b.at[s, 0]))
    pl.when(edge_a)(lambda: wait_bytes(idx_rows, send_i.at[0]))
    pl.when(edge_b)(lambda: wait_bytes(idx_rows.at[pl.ds(0, n_lon // 2)], send_i.at[1]))


def solution(mesh):
    n_lat, n_lon = mesh.shape["lat"], mesh.shape["lon"]

    def per_device(state, source_slot, donor_cell, donor_frac, donor_turn):
        _, comps, levels, rows, cols = state.shape
        f32, i32, dma = jnp.float32, jnp.int32, pltpu.SemaphoreType.DMA
        vmem = pl.BlockSpec(memory_space=pltpu.VMEM)
        return pl.pallas_call(
            functools.partial(kernel, n_lat, n_lon),
            out_shape=jax.ShapeDtypeStruct(state.shape, f32),
            in_specs=[pl.BlockSpec(memory_space=pltpu.HBM)] * 5,
            out_specs=vmem,
            scratch_shapes=[
                pltpu.VMEM((2, comps, levels, rows + 2 * PAD, cols), f32),
                pltpu.VMEM((1, donor_cell.shape[3]), i32),
                pltpu.VMEM((1, donor_cell.shape[3]), f32),
                pltpu.VMEM((2, donor_cell.shape[3]), f32),
                pltpu.VMEM((8, cols), i32),
                pltpu.VMEM((8, cols), f32),
                pltpu.VMEM((2, rows, cols), f32),
                pltpu.VMEM((2, 2, rows, cols), f32),
                pltpu.VMEM((2, n_lat, 8, cols), f32),
                pltpu.VMEM((n_lon, 1, 2 * cols), i32),
                pltpu.VMEM((2, 1, 2 * rows), i32),
                pltpu.VMEM((2, n_lon, 2, levels, 8, cols), f32),
                pltpu.VMEM((2, 2, levels, 8, cols), f32),
                pltpu.VMEM((2, n_lon, 2, levels, 8, cols), f32),
                pltpu.VMEM((2, n_lon, levels, 8, cols), f32),
                pltpu.VMEM((cols, cols), f32),
                dma((4,)),
                dma((2,)),
                dma((2,)),
                dma((2, 4)),
                dma((2, 4)),
                dma((2,)),
                dma((2,)),
                dma((2, 2)),
                dma((2, 2)),
            ],
            compiler_params=pltpu.CompilerParams(
                collective_id=0, has_side_effects=True, vmem_limit_bytes=62 * 2**20
            ),
        )(state, source_slot, donor_cell, donor_frac, donor_turn)

    in_specs = (
        P("panel", None, None, "lat", "lon"),
        P("panel", "lat", "lon", None),
        P("panel", "lat", "lon", None),
        P("panel", "lat", "lon", None, None),
        P("panel", "lat", "lon", None),
    )
    out_specs = P("panel", None, None, "lat", "lon")
    return jax.shard_map(
        per_device, mesh=mesh, in_specs=in_specs, out_specs=out_specs, check_vma=False
    )
```

```python
import functools

import jax
import jax.numpy as jnp
from jax import lax
from jax.experimental import pallas as pl
from jax.experimental.pallas import tpu as pltpu
from jax.sharding import PartitionSpec as P

MESH = pl.DeviceIdType.MESH
DIFFUSION = 0.05
BUOYANCY = 0.5
STEP = 0.25
PAD = 8
UP, DOWN, LEFT, RIGHT = range(4)


def row_order(n_lon):
    ways = sorted(range(n_lon), key=lambda d: -(2 if d & 6 == 4 else 1 if d & 6 else 0))
    return [ways[i : i + 4] for i in range(0, n_lon, 4)]


def pick_at(index, values):
    result = values[-1]
    for i, value in enumerate(values[:-1]):
        result = jnp.where(index == i, value, result)
    return result


def lane_take(value, index):
    return jnp.take_along_axis(value, index, axis=1, mode="promise_in_bounds")


def kernel(
    n_lat, n_lon, state, slots, cell, frac, turn, out,
    ext, cell_at, turn_at, frac_at, whole_i, whole_f, rows_to, rows_from, pack, pack_from, gathered, idx_rows, idx_sides,
    row_parts, side_parts, row_rim, side_rim, flip,
    load_sem, send_a, recv_a, send_h, recv_h, send_i, recv_i, send_b, recv_b,
):
    comps, levels, rows, cols = state.shape[1:]
    n_slots = cell.shape[3]
    half = cols // 2
    p = lax.axis_index("panel")
    a = lax.axis_index("lat")
    b = lax.axis_index("lon")
    other = 1 - p
    first_a, last_a = a == 0, a == n_lat - 1
    first_b, last_b = b == 0, b == n_lon - 1
    edge_a = jnp.logical_or(first_a, last_a)
    edge_b = jnp.logical_or(first_b, last_b)
    edge = jnp.logical_or(edge_a, edge_b)

    neighbours = (
        (a > 0, (p, a - 1, b)),
        (a < n_lat - 1, (p, a + 1, b)),
        (b > 0, (p, a, b - 1)),
        (b < n_lon - 1, (p, a, b + 1)),
    )

    loads = [
        pltpu.make_async_copy(cell.at[0, 0], cell_at, load_sem.at[1]),
        pltpu.make_async_copy(turn.at[0, 0], turn_at, load_sem.at[2]),
        pltpu.make_async_copy(frac.at[0, 0, 0], frac_at, load_sem.at[3]),
        pltpu.make_async_copy(
            state.at[0], ext.at[0, :, :, pl.ds(PAD, rows), :], load_sem.at[0]
        ),
    ]
    for load in loads:
        load.start()

    barrier = pltpu.get_barrier_semaphore()

    def greet(device):
        pl.semaphore_signal(barrier, inc=1, device_id=device, device_id_type=MESH)

    @pl.loop(0, n_lon)
    def _(k):
        greet((other, a, k))

    @pl.loop(1, n_lat)
    def _(k):
        greet((p, lax.rem(a + k, n_lat), b))

    for there, device in neighbours[2:]:
        pl.when(there)(functools.partial(greet, device))
    greeted = n_lon + n_lat - 1 + (b > 0).astype(jnp.int32) + (b < n_lon - 1).astype(jnp.int32)

    for load in loads[:3]:
        load.wait()
    whole_i[...] = jnp.zeros_like(whole_i)
    whole_f[...] = jnp.zeros_like(whole_f)
    for start in (0, half):
        whole_i[0:1, start : start + n_slots] = cell_at[...]
        whole_f[0:1, start : start + n_slots] = turn_at[...]
        whole_f[1:3, start : start + n_slots] = frac_at[...]
    cells = whole_i[0:1, :]
    turns = whole_f[0:1, :]
    cosine = jnp.cos(turns)
    sine = jnp.sin(turns)
    frac_t = whole_f[1:2, :]
    frac_p = whole_f[2:3, :]
    row = (cells * 33027) >> 22
    col = cells - row * (cols - 1)
    row_at = lax.broadcasted_iota(jnp.int32, (rows, cols), 0)
    row_full = jnp.broadcast_to(row, (rows, cols))
    weight_t = jnp.where(
        row_at == row_full,
        jnp.broadcast_to(1.0 - frac_t, (rows, cols)),
        jnp.where(row_at == row_full + 1, jnp.broadcast_to(frac_t, (rows, cols)), 0.0),
    )
    lane = lax.broadcasted_iota(jnp.int32, (rows, cols), 1)
    low_lane = lane < half
    lower_at = jnp.broadcast_to(col, (rows, cols))
    upper_at = lower_at + 1
    left_p = jnp.broadcast_to(1.0 - frac_p, (rows, cols))
    right_p = jnp.broadcast_to(frac_p, (rows, cols))

    def inner(s, c, level, shift=0):
        return ext[s, c, level, PAD + shift : PAD + shift + rows, :]

    def donate(s):
        given = []
        for c in range(comps):
            low, high = inner(s, c, 0), inner(s, c, 1)
            one = jnp.where(low_lane, lane_take(low, lower_at), lane_take(high, lower_at))
            two = jnp.where(low_lane, lane_take(low, upper_at), lane_take(high, upper_at))
            mixed = (left_p * one + right_p * two) * weight_t
            given.append(jnp.sum(mixed, axis=0, keepdims=True))
        for i in (1, 4):
            x, y = given[i], given[i + 1]
            given[i], given[i + 1] = cosine * x - sine * y, sine * x + cosine * y
        for c in range(comps):
            gathered[s, a, c : c + 1, :] = given[c]
        gathered[s, a, comps : comps + 1, :] = jnp.zeros((1, cols), jnp.float32)

    def pack_sides(s):
        packed = jnp.zeros((rows, cols), jnp.float32)
        for f in range(comps * levels):
            turned = pltpu.roll(inner(s, f // levels, f % levels), 4 * f + 2, 1)
            packed = jnp.where(lane >> 2 == f, turned, packed)
        pack[s] = packed

    def pack_rows(s):
        for f in range(comps * levels):
            c, level = f // levels, f % levels
            rows_to[s, 0, f] = ext[s, c, level, PAD : PAD + 2, :]
            rows_to[s, 1, f] = ext[s, c, level, PAD + rows - 2 : PAD + rows, :]

    def halo_copies(s):
        pairs = (
            (rows_to.at[s, 0], rows_from.at[s, 1]),
            (rows_to.at[s, 1], rows_from.at[s, 0]),
            (pack.at[s], pack_from.at[s, 1]),
            (pack.at[s], pack_from.at[s, 0]),
        )
        copies = []
        for to, (src, dst) in enumerate(pairs):
            copies.append(
                pltpu.make_async_remote_copy(
                    src_ref=src,
                    dst_ref=dst,
                    send_sem=send_h.at[s, to],
                    recv_sem=recv_h.at[s, to],
                    device_id=neighbours[to][1],
                    device_id_type=MESH,
                )
            )
        return copies

    def wait_bytes(ref, sem):
        pltpu.make_async_copy(ref, ref, sem).wait()

    def start_halo(s):
        for (there, _), copy in zip(neighbours, halo_copies(s)):
            pl.when(there)(copy.start)

    def start_a(s):
        @pl.loop(0, n_lat - 1)
        def _(k):
            step = (k + 1) >> 1
            away = n_lat // 2 + jnp.where(k & 1 == 1, step, -step)
            pltpu.make_async_remote_copy(
                src_ref=gathered.at[s, a],
                dst_ref=gathered.at[s, a],
                send_sem=send_a.at[s],
                recv_sem=recv_a.at[s],
                device_id=(p, lax.rem(a + away, n_lat), b),
                device_id_type=MESH,
            ).start()

    def wait_a(s, sem):
        wait_bytes(gathered.at[s, pl.ds(0, n_lat - 1)], sem.at[s])

    def send_slots():
        def send(start, dst, kind):
            size = dst.shape[-1]

            @pl.loop(0, n_lon)
            def _(k):
                pltpu.make_async_remote_copy(
                    src_ref=slots.at[0, 0, :, pl.ds(start, size)],
                    dst_ref=dst,
                    send_sem=send_i.at[kind],
                    recv_sem=recv_i.at[kind],
                    device_id=(other, a, k),
                    device_id_type=MESH,
                ).start()

        pl.when(first_a)(lambda: send(0, idx_rows.at[b], 0))
        pl.when(last_a)(lambda: send(2 * cols, idx_rows.at[b], 0))
        pl.when(first_b)(lambda: send(4 * cols, idx_sides.at[0], 1))
        pl.when(last_b)(lambda: send(4 * cols + 2 * rows, idx_sides.at[1], 1))

    def wait_slots():
        pl.when(edge_a)(lambda: wait_bytes(idx_rows, recv_i.at[0]))
        wait_bytes(idx_sides, recv_i.at[1])

    def pick(s, wanted):
        device = ((wanted >> 4) * 21846) >> 16
        place = jnp.broadcast_to(wanted - device * n_slots, (8, cols))
        row_of = device >> (n_lon.bit_length() - 1)
        giver = jnp.where(device - row_of * n_lon == b, row_of, -1)
        giver = jnp.broadcast_to(giver, (8, cols))
        totals = [jnp.zeros((8, cols), jnp.float32)] * levels
        places = [place + level * half for level in range(levels)]
        for k in range(n_lat):
            block = gathered[s, k]
            mine = giver == k
            for level in range(levels):
                totals[level] = jnp.where(mine, lane_take(block, places[level]), totals[level])
        return totals

    def send_parts(s):
        def to(src, dst, kind, k):
            return pltpu.make_async_remote_copy(
                src_ref=src,
                dst_ref=dst.at[s, b],
                send_sem=send_b.at[s, kind],
                recv_sem=recv_b.at[s, kind],
                device_id=(other, a, k),
                device_id_type=MESH,
            )

        for side in range(2):
            for level, total in enumerate(pick(s, idx_sides[side])):
                side_parts[s, side, level] = total
            to(side_parts.at[s, side], side_rim, 1, side * (n_lon - 1)).start()

        @pl.when(edge_a)
        def _():
            order = row_order(n_lon)

            @pl.loop(0, len(order))
            def _(group):
                to_whom = [b ^ pick_at(group, way) for way in zip(*order)]
                for k in to_whom:
                    for t in range(2):
                        for level, total in enumerate(
                            pick(s, idx_rows[k, :, t * cols : (t + 1) * cols])
                        ):
                            row_parts[s, k, t, level] = total
                for k in to_whom:
                    to(row_parts.at[s, k], row_rim, 0, k).start()

    def take_rim(s):
        @pl.when(edge_a)
        def _():
            wait_bytes(row_rim.at[s], recv_b.at[s, 0])
            total = jnp.sum(row_rim[s], axis=0)

            def put(at):
                for t in range(2):
                    for level in range(levels):
                        for c in range(comps):
                            ext[s, c, level, at + t : at + t + 1, :] = total[t, level, c : c + 1, :]

            pl.when(first_a)(lambda: put(PAD - 2))
            pl.when(last_a)(lambda: put(PAD + rows))

        @pl.when(edge_b)
        def _():
            wait_bytes(side_rim.at[s], recv_b.at[s, 1])
            total = jnp.sum(side_rim[s], axis=0)

            def put(side):
                flip[...] = jnp.zeros_like(flip)
                for level in range(levels):
                    both = (total[level], pltpu.roll(total[level], half, 1))
                    for t in range(2):
                        for c in range(comps):
                            at = 4 * (c * levels + level) + 2 * side + t
                            flip[at : at + 1, :] = both[t][c : c + 1, :]
                pack_from[s, side] = flip[...].T[0:rows, :]

            pl.when(first_b)(lambda: put(0))
            pl.when(last_b)(lambda: put(1))

    def wait_halo(s):
        landed = (rows_from.at[s, 0], rows_from.at[s, 1], pack_from.at[s, 0], pack_from.at[s, 1])
        for side_of, opposite in ((UP, DOWN), (DOWN, UP), (LEFT, RIGHT), (RIGHT, LEFT)):

            @pl.when(neighbours[side_of][0])
            def _():
                wait_bytes(landed[side_of], recv_h.at[s, opposite])
                if side_of in (UP, DOWN):
                    at = PAD - 2 if side_of == UP else PAD + rows
                    for f in range(comps * levels):
                        ext[s, f // levels, f % levels, at : at + 2, :] = rows_from[s, side_of, f]

    def rates(s, emit, low_row=0, count=0):
        chunk = count or rows
        for base in (low_row,):
            lanes = lane[0:chunk]
            beside = jnp.where(
                lanes & 2 == 0,
                pack_from[s, 0, base : base + chunk, :],
                pack_from[s, 1, base : base + chunk, :],
            )

            def at(c, level, shift=0):
                low = PAD + base + shift
                return ext[s, c, level, low : low + chunk, :]

            for level in range(levels):
                u1, u2 = at(1, level) * (1.0 / 12.0), at(2, level) * (1.0 / 12.0)
                b1, b2 = at(4, level) * (1.0 / 12.0), at(5, level) * (1.0 / 12.0)

                def terms(c, with_b):
                    mid = at(c, level)
                    around = pltpu.roll(beside, (cols - 2 - 4 * (c * levels + level)) % cols, 1)
                    west1 = pltpu.roll(jnp.where(lanes == cols - 1, around, mid), 1, 1)
                    west2 = pltpu.roll(jnp.where(lanes >= cols - 2, around, mid), 2, 1)
                    east1 = pltpu.roll(jnp.where(lanes == 0, around, mid), cols - 1, 1)
                    east2 = pltpu.roll(jnp.where(lanes < 2, around, mid), cols - 2, 1)
                    north1, south1 = at(c, level, -1), at(c, level, 1)
                    d_lat = 8.0 * (south1 - north1) - (at(c, level, 2) - at(c, level, -2))
                    d_lon = 8.0 * (east1 - west1) - (east2 - west2)
                    lap = south1 + north1 + east1 + west1 + at(c, 1 - level) - 6.0 * mid
                    adv_u = u1 * d_lat + u2 * d_lon
                    adv_b = b1 * d_lat + b2 * d_lon if with_b else None
                    return mid, adv_u, adv_b, DIFFUSION * lap

                for c in range(3):
                    mid, adv_u, adv_b, lap = terms(c, True)
                    mid_b, adv_ub, adv_bb, lap_b = terms(c + 3, True)
                    moment = adv_bb - adv_u + lap
                    if c == 0:
                        moment = moment + BUOYANCY * at(6, level)
                    emit(c, level, base, mid, moment)
                    emit(c + 3, level, base, mid_b, adv_b - adv_ub + lap_b)
                mid, adv_u, _, lap = terms(6, False)
                emit(6, level, base, mid, lap - adv_u)

    def first_section(c, level, base, mid, rate):
        ext[1, c, level, PAD + base : PAD + base + mid.shape[0], :] = mid + STEP * rate

    def second_section(c, level, base, mid, rate):
        start = ext[0, c, level, PAD + base : PAD + base + mid.shape[0], :]
        out[0, c, level, base : base + mid.shape[0], :] = 0.5 * start + 0.5 * (mid + STEP * rate)

    def give(s):
        donate(s)
        if s == 0:
            pl.semaphore_wait(barrier, greeted)
        start_a(s)
        if s == 0:
            send_slots()
        pack_sides(s)
        pack_rows(s)
        start_halo(s)

    def mend(s, emit):
        take_rim(s)
        inside = jnp.logical_not(edge_b)
        pl.when(jnp.logical_and(first_a, inside))(lambda: rates(s, emit, 0, 8))
        pl.when(jnp.logical_and(last_a, inside))(lambda: rates(s, emit, rows - 8, 8))
        pl.when(edge_b)(lambda: rates(s, emit))

    loads[3].wait()
    give(0)
    wait_halo(0)
    rates(0, first_section)
    pl.when(jnp.logical_not(edge))(lambda: give(1))
    wait_a(0, recv_a)
    wait_slots()
    send_parts(0)

    @pl.when(edge)
    def _():
        mend(0, first_section)
        give(1)

    wait_halo(1)
    rates(1, second_section)
    wait_a(1, recv_a)
    send_parts(1)
    pl.when(edge)(lambda: mend(1, second_section))

    for s in range(2):
        wait_a(s, send_a)
        for (there, _), copy in zip(neighbours, halo_copies(s)):
            pl.when(there)(copy.wait_send)
        wait_bytes(side_parts.at[s], send_b.at[s, 1])
        pl.when(edge_a)(functools.partial(wait_bytes, row_parts.at[s], send_b.at[s, 0]))
    pl.when(edge_a)(lambda: wait_bytes(idx_rows, send_i.at[0]))
    pl.when(edge_b)(lambda: wait_bytes(idx_rows.at[pl.ds(0, n_lon // 2)], send_i.at[1]))


def solution(mesh):
    n_lat, n_lon = mesh.shape["lat"], mesh.shape["lon"]

    def per_device(state, source_slot, donor_cell, donor_frac, donor_turn):
        _, comps, levels, rows, cols = state.shape
        f32, i32, dma = jnp.float32, jnp.int32, pltpu.SemaphoreType.DMA
        vmem = pl.BlockSpec(memory_space=pltpu.VMEM)
        return pl.pallas_call(
            functools.partial(kernel, n_lat, n_lon),
            out_shape=jax.ShapeDtypeStruct(state.shape, f32),
            in_specs=[pl.BlockSpec(memory_space=pltpu.HBM)] * 5,
            out_specs=vmem,
            scratch_shapes=[
                pltpu.VMEM((2, comps, levels, rows + 2 * PAD, cols), f32),
                pltpu.VMEM((1, donor_cell.shape[3]), i32),
                pltpu.VMEM((1, donor_cell.shape[3]), f32),
                pltpu.VMEM((2, donor_cell.shape[3]), f32),
                pltpu.VMEM((8, cols), i32),
                pltpu.VMEM((8, cols), f32),
                pltpu.VMEM((2, 2, comps * levels, 2, cols), f32),
                pltpu.VMEM((2, 2, comps * levels, 2, cols), f32),
                pltpu.VMEM((2, rows, cols), f32),
                pltpu.VMEM((2, 2, rows, cols), f32),
                pltpu.VMEM((2, n_lat, 8, cols), f32),
                pltpu.VMEM((n_lon, 1, 2 * cols), i32),
                pltpu.VMEM((2, 1, 2 * rows), i32),
                pltpu.VMEM((2, n_lon, 2, levels, 8, cols), f32),
                pltpu.VMEM((2, 2, levels, 8, cols), f32),
                pltpu.VMEM((2, n_lon, 2, levels, 8, cols), f32),
                pltpu.VMEM((2, n_lon, levels, 8, cols), f32),
                pltpu.VMEM((cols, cols), f32),
                dma((4,)),
                dma((2,)),
                dma((2,)),
                dma((2, 4)),
                dma((2, 4)),
                dma((2,)),
                dma((2,)),
                dma((2, 2)),
                dma((2, 2)),
            ],
            compiler_params=pltpu.CompilerParams(
                collective_id=0, has_side_effects=True, vmem_limit_bytes=32 * 2**20
            ),
        )(
            *(
                pltpu.with_memory_space_constraint(x, pltpu.HBM)
                for x in (state, source_slot, donor_cell, donor_frac, donor_turn)
            )
        )

    in_specs = (
        P("panel", None, None, "lat", "lon"),
        P("panel", "lat", "lon", None),
        P("panel", "lat", "lon", None),
        P("panel", "lat", "lon", None, None),
        P("panel", "lat", "lon", None),
    )
    out_specs = P("panel", None, None, "lat", "lon")
    return jax.shard_map(
        per_device, mesh=mesh, in_specs=in_specs, out_specs=out_specs, check_vma=False
    )
```

```python
import functools

import jax
import jax.numpy as jnp
from jax import lax
from jax.experimental import pallas as pl
from jax.experimental.pallas import tpu as pltpu
from jax.sharding import PartitionSpec as P

MESH = pl.DeviceIdType.MESH
DIFFUSION = 0.05
BUOYANCY = 0.5
STEP = 0.25
PAD = 8
UP, DOWN, LEFT, RIGHT = range(4)


def row_order(n_lon):
    ways = sorted(range(n_lon), key=lambda d: -(2 if d & 6 == 4 else 1 if d & 6 else 0))
    return [ways[i : i + 4] for i in range(0, n_lon, 4)]


def pick_at(index, values):
    result = values[-1]
    for i, value in enumerate(values[:-1]):
        result = jnp.where(index == i, value, result)
    return result


def lane_take(value, index):
    return jnp.take_along_axis(value, index, axis=1, mode="promise_in_bounds")


def kernel(
    n_lat, n_lon, state, slots, cell, frac, turn, out,
    ext, cell_at, turn_at, frac_at, whole_i, whole_f, rows_to, rows_from, pack, pack_from, gathered, dense, idx_rows, idx_sides,
    row_parts, side_parts, row_rim, side_rim, flip,
    load_sem, send_a, recv_a, send_h, recv_h, send_i, recv_i, send_b, recv_b,
):
    comps, levels, rows, cols = state.shape[1:]
    n_slots = cell.shape[3]
    half = cols // 2
    p = lax.axis_index("panel")
    a = lax.axis_index("lat")
    b = lax.axis_index("lon")
    other = 1 - p
    first_a, last_a = a == 0, a == n_lat - 1
    first_b, last_b = b == 0, b == n_lon - 1
    edge_a = jnp.logical_or(first_a, last_a)
    edge_b = jnp.logical_or(first_b, last_b)
    edge = jnp.logical_or(edge_a, edge_b)

    neighbours = (
        (a > 0, (p, a - 1, b)),
        (a < n_lat - 1, (p, a + 1, b)),
        (b > 0, (p, a, b - 1)),
        (b < n_lon - 1, (p, a, b + 1)),
    )

    loads = [
        pltpu.make_async_copy(cell.at[0, 0], cell_at, load_sem.at[1]),
        pltpu.make_async_copy(turn.at[0, 0], turn_at, load_sem.at[2]),
        pltpu.make_async_copy(frac.at[0, 0, 0], frac_at, load_sem.at[3]),
        pltpu.make_async_copy(
            state.at[0], ext.at[0, :, :, pl.ds(PAD, rows), :], load_sem.at[0]
        ),
    ]
    for load in loads:
        load.start()

    barrier = pltpu.get_barrier_semaphore()

    def greet(device):
        pl.semaphore_signal(barrier, inc=1, device_id=device, device_id_type=MESH)

    @pl.loop(0, n_lon)
    def _(k):
        greet((other, a, k))

    @pl.loop(1, n_lat)
    def _(k):
        greet((p, lax.rem(a + k, n_lat), b))

    for there, device in neighbours[2:]:
        pl.when(there)(functools.partial(greet, device))
    greeted = n_lon + n_lat - 1 + (b > 0).astype(jnp.int32) + (b < n_lon - 1).astype(jnp.int32)

    for load in loads[:3]:
        load.wait()
    whole_i[...] = jnp.zeros_like(whole_i)
    whole_f[...] = jnp.zeros_like(whole_f)
    for start in (0, half):
        whole_i[0:1, start : start + n_slots] = cell_at[...]
        whole_f[0:1, start : start + n_slots] = turn_at[...]
        whole_f[1:3, start : start + n_slots] = frac_at[...]
    cells = whole_i[0:1, :]
    turns = whole_f[0:1, :]
    cosine = jnp.cos(turns)
    sine = jnp.sin(turns)
    frac_t = whole_f[1:2, :]
    frac_p = whole_f[2:3, :]
    row = (cells * 33027) >> 22
    col = cells - row * (cols - 1)
    row_at = lax.broadcasted_iota(jnp.int32, (rows, cols), 0)
    row_full = jnp.broadcast_to(row, (rows, cols))
    weight_t = jnp.where(
        row_at == row_full,
        jnp.broadcast_to(1.0 - frac_t, (rows, cols)),
        jnp.where(row_at == row_full + 1, jnp.broadcast_to(frac_t, (rows, cols)), 0.0),
    )
    lane = lax.broadcasted_iota(jnp.int32, (rows, cols), 1)
    low_lane = lane < half
    col_at = jnp.broadcast_to(col, (rows, cols)) + jnp.where(low_lane, 0, 1)
    weight = weight_t * jnp.where(
        low_lane,
        jnp.broadcast_to(1.0 - frac_p, (rows, cols)),
        jnp.broadcast_to(frac_p, (rows, cols)),
    )

    def inner(s, c, level, shift=0):
        return ext[s, c, level, PAD + shift : PAD + shift + rows, :]

    def donate(s):
        given = []
        for c in range(comps):
            sums = []
            for level in range(levels):
                halves = jnp.sum(lane_take(inner(s, c, level), col_at) * weight, axis=0, keepdims=True)
                sums.append(halves + pltpu.roll(halves, half, 1))
            given.append(jnp.where(low_lane[0:1], sums[0], sums[1]))
        for i in (1, 4):
            x, y = given[i], given[i + 1]
            given[i], given[i + 1] = cosine * x - sine * y, sine * x + cosine * y
        for c in range(comps):
            gathered[s, a, c : c + 1, :] = given[c]
        gathered[s, a, comps : comps + 1, :] = jnp.zeros((1, cols), jnp.float32)

    def pack_sides(s):
        packed = jnp.zeros((rows, cols), jnp.float32)
        for f in range(comps * levels):
            turned = pltpu.roll(inner(s, f // levels, f % levels), 4 * f + 2, 1)
            packed = jnp.where(lane >> 2 == f, turned, packed)
        pack[s] = packed

    def pack_rows(s):
        for f in range(comps * levels):
            c, level = f // levels, f % levels
            rows_to[s, 0, f] = ext[s, c, level, PAD : PAD + 2, :]
            rows_to[s, 1, f] = ext[s, c, level, PAD + rows - 2 : PAD + rows, :]

    def halo_copies(s):
        pairs = (
            (rows_to.at[s, 0], rows_from.at[s, 1]),
            (rows_to.at[s, 1], rows_from.at[s, 0]),
            (pack.at[s], pack_from.at[s, 1]),
            (pack.at[s], pack_from.at[s, 0]),
        )
        copies = []
        for to, (src, dst) in enumerate(pairs):
            copies.append(
                pltpu.make_async_remote_copy(
                    src_ref=src,
                    dst_ref=dst,
                    send_sem=send_h.at[s, to],
                    recv_sem=recv_h.at[s, to],
                    device_id=neighbours[to][1],
                    device_id_type=MESH,
                )
            )
        return copies

    def wait_bytes(ref, sem):
        pltpu.make_async_copy(ref, ref, sem).wait()

    def start_halo(s):
        for (there, _), copy in zip(neighbours, halo_copies(s)):
            pl.when(there)(copy.start)

    def start_a(s):
        @pl.loop(0, n_lat - 1)
        def _(k):
            step = (k + 1) >> 1
            away = n_lat // 2 + jnp.where(k & 1 == 1, step, -step)
            pltpu.make_async_remote_copy(
                src_ref=gathered.at[s, a],
                dst_ref=gathered.at[s, a],
                send_sem=send_a.at[s],
                recv_sem=recv_a.at[s],
                device_id=(p, lax.rem(a + away, n_lat), b),
                device_id_type=MESH,
            ).start()

    def wait_a(s, sem):
        wait_bytes(gathered.at[s, pl.ds(0, n_lat - 1)], sem.at[s])

    def send_slots():
        def send(start, dst, kind):
            size = dst.shape[-1]

            @pl.loop(0, n_lon)
            def _(k):
                pltpu.make_async_remote_copy(
                    src_ref=slots.at[0, 0, :, pl.ds(start, size)],
                    dst_ref=dst,
                    send_sem=send_i.at[kind],
                    recv_sem=recv_i.at[kind],
                    device_id=(other, a, k),
                    device_id_type=MESH,
                ).start()

        pl.when(first_a)(lambda: send(0, idx_rows.at[b], 0))
        pl.when(last_a)(lambda: send(2 * cols, idx_rows.at[b], 0))
        pl.when(first_b)(lambda: send(4 * cols, idx_sides.at[0], 1))
        pl.when(last_b)(lambda: send(4 * cols + 2 * rows, idx_sides.at[1], 1))

    def wait_slots():
        pl.when(edge_a)(lambda: wait_bytes(idx_rows, recv_i.at[0]))
        wait_bytes(idx_sides, recv_i.at[1])

    groups = -(-n_lat * n_slots // cols)
    lane8 = lane[0:8]

    def settle(s):
        for level in range(levels):
            totals = [jnp.zeros((8, cols), jnp.float32)] * groups
            for k in range(n_lat):
                low, high = k * n_slots, (k + 1) * n_slots
                turned = pltpu.roll(gathered[s, k], (low - level * half) % cols, 1)
                for g in range(low // cols, (high - 1) // cols + 1):
                    here = jnp.logical_and(lane8 >= low - g * cols, lane8 < high - g * cols)
                    totals[g] = jnp.where(here, turned, totals[g])
            for g in range(groups):
                dense[s, level, g] = totals[g]

    def pick(s, wanted):
        device = ((wanted >> 4) * 21846) >> 16
        row_of = device >> (n_lon.bit_length() - 1)
        number = wanted - (device - row_of) * n_slots
        group = jnp.where(device - row_of * n_lon == b, number >> (cols.bit_length() - 1), -1)
        group = jnp.broadcast_to(group, (8, cols))
        place = jnp.broadcast_to(number & (cols - 1), (8, cols))
        totals = [jnp.zeros((8, cols), jnp.float32)] * levels
        for g in range(groups):
            mine = group == g
            for level in range(levels):
                totals[level] = jnp.where(mine, lane_take(dense[s, level, g], place), totals[level])
        return totals

    def send_parts(s):
        def to(src, dst, kind, k):
            return pltpu.make_async_remote_copy(
                src_ref=src,
                dst_ref=dst.at[s, b],
                send_sem=send_b.at[s, kind],
                recv_sem=recv_b.at[s, kind],
                device_id=(other, a, k),
                device_id_type=MESH,
            )

        settle(s)
        for side in range(2):
            for level, total in enumerate(pick(s, idx_sides[side])):
                side_parts[s, side, level] = total
            to(side_parts.at[s, side], side_rim, 1, side * (n_lon - 1)).start()

        @pl.when(edge_a)
        def _():
            order = row_order(n_lon)

            @pl.loop(0, len(order))
            def _(group):
                to_whom = [b ^ pick_at(group, way) for way in zip(*order)]
                for k in to_whom:
                    for t in range(2):
                        for level, total in enumerate(
                            pick(s, idx_rows[k, :, t * cols : (t + 1) * cols])
                        ):
                            row_parts[s, k, t, level] = total
                for k in to_whom:
                    to(row_parts.at[s, k], row_rim, 0, k).start()

    def take_rim(s):
        @pl.when(edge_a)
        def _():
            wait_bytes(row_rim.at[s], recv_b.at[s, 0])
            total = jnp.sum(row_rim[s], axis=0)

            def put(at):
                for t in range(2):
                    for level in range(levels):
                        for c in range(comps):
                            ext[s, c, level, at + t : at + t + 1, :] = total[t, level, c : c + 1, :]

            pl.when(first_a)(lambda: put(PAD - 2))
            pl.when(last_a)(lambda: put(PAD + rows))

        @pl.when(edge_b)
        def _():
            wait_bytes(side_rim.at[s], recv_b.at[s, 1])
            total = jnp.sum(side_rim[s], axis=0)

            def put(side):
                flip[...] = jnp.zeros_like(flip)
                for level in range(levels):
                    both = (total[level], pltpu.roll(total[level], half, 1))
                    for t in range(2):
                        for c in range(comps):
                            at = 4 * (c * levels + level) + 2 * side + t
                            flip[at : at + 1, :] = both[t][c : c + 1, :]
                pack_from[s, side] = flip[...].T[0:rows, :]

            pl.when(first_b)(lambda: put(0))
            pl.when(last_b)(lambda: put(1))

    def wait_halo(s):
        landed = (rows_from.at[s, 0], rows_from.at[s, 1], pack_from.at[s, 0], pack_from.at[s, 1])
        for side_of, opposite in ((UP, DOWN), (DOWN, UP), (LEFT, RIGHT), (RIGHT, LEFT)):

            @pl.when(neighbours[side_of][0])
            def _():
                wait_bytes(landed[side_of], recv_h.at[s, opposite])
                if side_of in (UP, DOWN):
                    at = PAD - 2 if side_of == UP else PAD + rows
                    for f in range(comps * levels):
                        ext[s, f // levels, f % levels, at : at + 2, :] = rows_from[s, side_of, f]

    def rates(s, emit, low_row=0, count=0):
        chunk = count or rows
        for base in (low_row,):
            lanes = lane[0:chunk]
            beside = jnp.where(
                lanes & 2 == 0,
                pack_from[s, 0, base : base + chunk, :],
                pack_from[s, 1, base : base + chunk, :],
            )

            def at(c, level, shift=0):
                low = PAD + base + shift
                return ext[s, c, level, low : low + chunk, :]

            for level in range(levels):
                u1, u2 = at(1, level) * (1.0 / 12.0), at(2, level) * (1.0 / 12.0)
                b1, b2 = at(4, level) * (1.0 / 12.0), at(5, level) * (1.0 / 12.0)

                def terms(c, with_b):
                    mid = at(c, level)
                    around = pltpu.roll(beside, (cols - 2 - 4 * (c * levels + level)) % cols, 1)
                    west1 = pltpu.roll(jnp.where(lanes == cols - 1, around, mid), 1, 1)
                    west2 = pltpu.roll(jnp.where(lanes >= cols - 2, around, mid), 2, 1)
                    east1 = pltpu.roll(jnp.where(lanes == 0, around, mid), cols - 1, 1)
                    east2 = pltpu.roll(jnp.where(lanes < 2, around, mid), cols - 2, 1)
                    north1, south1 = at(c, level, -1), at(c, level, 1)
                    d_lat = 8.0 * (south1 - north1) - (at(c, level, 2) - at(c, level, -2))
                    d_lon = 8.0 * (east1 - west1) - (east2 - west2)
                    lap = south1 + north1 + east1 + west1 + at(c, 1 - level) - 6.0 * mid
                    adv_u = u1 * d_lat + u2 * d_lon
                    adv_b = b1 * d_lat + b2 * d_lon if with_b else None
                    return mid, adv_u, adv_b, DIFFUSION * lap

                for c in range(3):
                    mid, adv_u, adv_b, lap = terms(c, True)
                    mid_b, adv_ub, adv_bb, lap_b = terms(c + 3, True)
                    moment = adv_bb - adv_u + lap
                    if c == 0:
                        moment = moment + BUOYANCY * at(6, level)
                    emit(c, level, base, mid, moment)
                    emit(c + 3, level, base, mid_b, adv_b - adv_ub + lap_b)
                mid, adv_u, _, lap = terms(6, False)
                emit(6, level, base, mid, lap - adv_u)

    def first_section(c, level, base, mid, rate):
        ext[1, c, level, PAD + base : PAD + base + mid.shape[0], :] = mid + STEP * rate

    def second_section(c, level, base, mid, rate):
        start = ext[0, c, level, PAD + base : PAD + base + mid.shape[0], :]
        out[0, c, level, base : base + mid.shape[0], :] = 0.5 * start + 0.5 * (mid + STEP * rate)

    def give(s):
        donate(s)
        if s == 0:
            pl.semaphore_wait(barrier, greeted)
        start_a(s)
        if s == 0:
            send_slots()
        pack_sides(s)
        pack_rows(s)
        start_halo(s)

    def mend_side(s):
        rim = jnp.where(first_b, pack_from[s, 0], pack_from[s, 1])
        spot = lane & 3
        near_w, far_w = pltpu.roll(rim, 1, 1), pltpu.roll(rim, 2, 1)
        near_e, far_e = pltpu.roll(rim, cols - 1, 1), pltpu.roll(rim, cols - 2, 1)
        slope = jnp.where(
            spot == 2,
            far_w - 8.0 * near_w,
            jnp.where(spot == 3, far_w, jnp.where(spot == 1, 8.0 * near_e - far_e, -far_e)),
        ) * (1.0 / 12.0)
        lap = jnp.where(spot == 2, near_w, jnp.where(spot == 1, near_e, 0.0))
        per_comp = 4 * levels
        within = lane & (per_comp - 1)
        u2 = lane_take(pack[s], within + 2 * per_comp)
        b2 = lane_take(pack[s], within + 5 * per_comp)
        swap = 3 * per_comp
        partner = jnp.where(
            lane < swap,
            pltpu.roll(slope, cols - swap, 1),
            jnp.where(lane < 2 * swap, pltpu.roll(slope, swap, 1), 0.0),
        )
        scale = STEP if s == 0 else 0.5 * STEP
        change = scale * (DIFFUSION * lap - u2 * slope + b2 * partner)
        outer = jnp.logical_or(lane >= cols - 2, lane < 2)
        for f in range(comps * levels):
            c, level = f // levels, f % levels
            here = jnp.where(outer, pltpu.roll(change, (cols - 2 - 4 * f) % cols, 1), 0.0)
            if s == 0:
                ext[1, c, level, PAD : PAD + rows, :] = inner(1, c, level) + here
            else:
                out[0, c, level] = out[0, c, level] + here

    def mend(s, emit):
        take_rim(s)
        pl.when(edge_b)(lambda: mend_side(s))
        pl.when(first_a)(lambda: rates(s, emit, 0, 8))
        pl.when(last_a)(lambda: rates(s, emit, rows - 8, 8))

    for s in range(2):

        @pl.when(first_b)
        def _():
            pack_from[s, 0] = jnp.zeros((rows, cols), jnp.float32)

        @pl.when(last_b)
        def _():
            pack_from[s, 1] = jnp.zeros((rows, cols), jnp.float32)

    loads[3].wait()
    give(0)
    wait_halo(0)
    rates(0, first_section)
    wait_a(0, recv_a)
    wait_slots()
    send_parts(0)

    pl.when(edge)(lambda: mend(0, first_section))
    give(1)

    wait_halo(1)
    rates(1, second_section)
    wait_a(1, recv_a)
    send_parts(1)
    pl.when(edge)(lambda: mend(1, second_section))

    for s in range(2):
        wait_a(s, send_a)
        for (there, _), copy in zip(neighbours, halo_copies(s)):
            pl.when(there)(copy.wait_send)
        wait_bytes(side_parts.at[s], send_b.at[s, 1])
        pl.when(edge_a)(functools.partial(wait_bytes, row_parts.at[s], send_b.at[s, 0]))
    pl.when(edge_a)(lambda: wait_bytes(idx_rows, send_i.at[0]))
    pl.when(edge_b)(lambda: wait_bytes(idx_rows.at[pl.ds(0, n_lon // 2)], send_i.at[1]))


def solution(mesh):
    n_lat, n_lon = mesh.shape["lat"], mesh.shape["lon"]

    def per_device(state, source_slot, donor_cell, donor_frac, donor_turn):
        _, comps, levels, rows, cols = state.shape
        f32, i32, dma = jnp.float32, jnp.int32, pltpu.SemaphoreType.DMA
        vmem = pl.BlockSpec(memory_space=pltpu.VMEM)
        return pl.pallas_call(
            functools.partial(kernel, n_lat, n_lon),
            out_shape=jax.ShapeDtypeStruct(state.shape, f32),
            in_specs=[pl.BlockSpec(memory_space=pltpu.HBM)] * 5,
            out_specs=vmem,
            scratch_shapes=[
                pltpu.VMEM((2, comps, levels, rows + 2 * PAD, cols), f32),
                pltpu.VMEM((1, donor_cell.shape[3]), i32),
                pltpu.VMEM((1, donor_cell.shape[3]), f32),
                pltpu.VMEM((2, donor_cell.shape[3]), f32),
                pltpu.VMEM((8, cols), i32),
                pltpu.VMEM((8, cols), f32),
                pltpu.VMEM((2, 2, comps * levels, 2, cols), f32),
                pltpu.VMEM((2, 2, comps * levels, 2, cols), f32),
                pltpu.VMEM((2, rows, cols), f32),
                pltpu.VMEM((2, 2, rows, cols), f32),
                pltpu.VMEM((2, n_lat, 8, cols), f32),
                pltpu.VMEM((2, levels, -(-n_lat * donor_cell.shape[3] // cols), 8, cols), f32),
                pltpu.VMEM((n_lon, 1, 2 * cols), i32),
                pltpu.VMEM((2, 1, 2 * rows), i32),
                pltpu.VMEM((2, n_lon, 2, levels, 8, cols), f32),
                pltpu.VMEM((2, 2, levels, 8, cols), f32),
                pltpu.VMEM((2, n_lon, 2, levels, 8, cols), f32),
                pltpu.VMEM((2, n_lon, levels, 8, cols), f32),
                pltpu.VMEM((cols, cols), f32),
                dma((4,)),
                dma((2,)),
                dma((2,)),
                dma((2, 4)),
                dma((2, 4)),
                dma((2,)),
                dma((2,)),
                dma((2, 2)),
                dma((2, 2)),
            ],
            compiler_params=pltpu.CompilerParams(
                collective_id=0, has_side_effects=True, vmem_limit_bytes=32 * 2**20
            ),
        )(
            *(
                pltpu.with_memory_space_constraint(x, pltpu.HBM)
                for x in (state, source_slot, donor_cell, donor_frac, donor_turn)
            )
        )

    in_specs = (
        P("panel", None, None, "lat", "lon"),
        P("panel", "lat", "lon", None),
        P("panel", "lat", "lon", None),
        P("panel", "lat", "lon", None, None),
        P("panel", "lat", "lon", None),
    )
    out_specs = P("panel", None, None, "lat", "lon")
    return jax.shard_map(
        per_device, mesh=mesh, in_specs=in_specs, out_specs=out_specs, check_vma=False
    )
```

```python
import functools

import jax
import jax.numpy as jnp
from jax import lax
from jax.experimental import pallas as pl
from jax.experimental.pallas import tpu as pltpu
from jax.sharding import PartitionSpec as P

MESH = pl.DeviceIdType.MESH
DIFFUSION = 0.05
BUOYANCY = 0.5
STEP = 0.25
PAD = 8
UP, DOWN, LEFT, RIGHT = range(4)


def row_order(n_lon):
    ways = sorted(range(n_lon), key=lambda d: -(2 if d & 6 == 4 else 1 if d & 6 else 0))
    return [ways[i : i + 4] for i in range(0, n_lon, 4)]


def pick_at(index, values):
    result = values[-1]
    for i, value in enumerate(values[:-1]):
        result = jnp.where(index == i, value, result)
    return result


def lane_take(value, index):
    return jnp.take_along_axis(value, index, axis=1, mode="promise_in_bounds")


def kernel(
    n_lat, n_lon, state, slots, cell, frac, turn, out,
    ext, cell_at, turn_at, frac_at, whole_i, whole_f, rows_to, rows_from, pack, pack_from, gathered, dense, idx_rows, idx_sides,
    row_parts, side_parts, row_rim, side_rim, flip,
    load_sem, send_a, recv_a, send_h, recv_h, send_i, recv_i, send_b, recv_b,
):
    comps, levels, rows, cols = state.shape[1:]
    n_slots = cell.shape[3]
    half = cols // 2
    p = lax.axis_index("panel")
    a = lax.axis_index("lat")
    b = lax.axis_index("lon")
    other = 1 - p
    first_a, last_a = a == 0, a == n_lat - 1
    first_b, last_b = b == 0, b == n_lon - 1
    edge_a = jnp.logical_or(first_a, last_a)
    edge_b = jnp.logical_or(first_b, last_b)
    edge = jnp.logical_or(edge_a, edge_b)

    neighbours = (
        (a > 0, (p, a - 1, b)),
        (a < n_lat - 1, (p, a + 1, b)),
        (b > 0, (p, a, b - 1)),
        (b < n_lon - 1, (p, a, b + 1)),
    )

    loads = [
        pltpu.make_async_copy(cell.at[0, 0], cell_at, load_sem.at[1]),
        pltpu.make_async_copy(turn.at[0, 0], turn_at, load_sem.at[2]),
        pltpu.make_async_copy(frac.at[0, 0, 0], frac_at, load_sem.at[3]),
        pltpu.make_async_copy(
            state.at[0], ext.at[0, :, :, pl.ds(PAD, rows), :], load_sem.at[0]
        ),
    ]
    for load in loads:
        load.start()

    def far_first(k):
        step = (k + 1) >> 1
        return n_lat // 2 + jnp.where(k & 1 == 1, step, -step)

    barrier = pltpu.get_barrier_semaphore()

    def greet(device):
        pl.semaphore_signal(barrier, inc=1, device_id=device, device_id_type=MESH)

    @pl.loop(0, n_lat - 1)
    def _(k):
        greet((p, lax.rem(a + far_first(k), n_lat), b))

    @pl.loop(0, n_lon)
    def _(k):
        greet((other, a, k))

    for there, device in neighbours[2:]:
        pl.when(there)(functools.partial(greet, device))
    greeted = n_lon + n_lat - 1 + (b > 0).astype(jnp.int32) + (b < n_lon - 1).astype(jnp.int32)

    for load in loads[:3]:
        load.wait()
    whole_i[...] = jnp.zeros_like(whole_i)
    whole_f[...] = jnp.zeros_like(whole_f)
    for start in (0, half):
        whole_i[0:1, start : start + n_slots] = cell_at[...]
        whole_f[0:1, start : start + n_slots] = turn_at[...]
        whole_f[1:3, start : start + n_slots] = frac_at[...]
    cells = whole_i[0:1, :]
    turns = whole_f[0:1, :]
    cosine = jnp.cos(turns)
    sine = jnp.sin(turns)
    frac_t = whole_f[1:2, :]
    frac_p = whole_f[2:3, :]
    row = (cells * 33027) >> 22
    col = cells - row * (cols - 1)
    row_at = lax.broadcasted_iota(jnp.int32, (rows, cols), 0)
    row_full = jnp.broadcast_to(row, (rows, cols))
    weight_t = jnp.where(
        row_at == row_full,
        jnp.broadcast_to(1.0 - frac_t, (rows, cols)),
        jnp.where(row_at == row_full + 1, jnp.broadcast_to(frac_t, (rows, cols)), 0.0),
    )
    lane = lax.broadcasted_iota(jnp.int32, (rows, cols), 1)
    low_lane = lane < half
    col_at = jnp.broadcast_to(col, (rows, cols)) + jnp.where(low_lane, 0, 1)
    weight = weight_t * jnp.where(
        low_lane,
        jnp.broadcast_to(1.0 - frac_p, (rows, cols)),
        jnp.broadcast_to(frac_p, (rows, cols)),
    )

    def inner(s, c, level, shift=0):
        return ext[s, c, level, PAD + shift : PAD + shift + rows, :]

    def donate(s):
        given = []
        for c in range(comps):
            sums = []
            for level in range(levels):
                halves = jnp.sum(lane_take(inner(s, c, level), col_at) * weight, axis=0, keepdims=True)
                sums.append(halves + pltpu.roll(halves, half, 1))
            given.append(jnp.where(low_lane[0:1], sums[0], sums[1]))
        for i in (1, 4):
            x, y = given[i], given[i + 1]
            given[i], given[i + 1] = cosine * x - sine * y, sine * x + cosine * y
        for c in range(comps):
            gathered[s, a, c : c + 1, :] = given[c]

    def pack_sides(s):
        packed = jnp.zeros((rows, cols), jnp.float32)
        for f in range(comps * levels):
            turned = pltpu.roll(inner(s, f // levels, f % levels), 4 * f + 2, 1)
            packed = jnp.where(lane >> 2 == f, turned, packed)
        pack[s] = packed

    def pack_rows(s):
        for f in range(comps * levels):
            c, level = f // levels, f % levels
            rows_to[s, 0, f] = ext[s, c, level, PAD : PAD + 2, :]
            rows_to[s, 1, f] = ext[s, c, level, PAD + rows - 2 : PAD + rows, :]

    def halo_copies(s):
        pairs = (
            (rows_to.at[s, 0], rows_from.at[s, 1]),
            (rows_to.at[s, 1], rows_from.at[s, 0]),
            (pack.at[s], pack_from.at[s, 1]),
            (pack.at[s], pack_from.at[s, 0]),
        )
        copies = []
        for to, (src, dst) in enumerate(pairs):
            copies.append(
                pltpu.make_async_remote_copy(
                    src_ref=src,
                    dst_ref=dst,
                    send_sem=send_h.at[s, to],
                    recv_sem=recv_h.at[s, to],
                    device_id=neighbours[to][1],
                    device_id_type=MESH,
                )
            )
        return copies

    def wait_bytes(ref, sem):
        pltpu.make_async_copy(ref, ref, sem).wait()

    def start_halo(s):
        for (there, _), copy in zip(neighbours, halo_copies(s)):
            pl.when(there)(copy.start)

    def start_a(s):
        @pl.loop(0, n_lat - 1)
        def _(k):
            pltpu.make_async_remote_copy(
                src_ref=gathered.at[s, a, pl.ds(0, comps)],
                dst_ref=gathered.at[s, a, pl.ds(0, comps)],
                send_sem=send_a.at[s],
                recv_sem=recv_a.at[s],
                device_id=(p, lax.rem(a + far_first(k), n_lat), b),
                device_id_type=MESH,
            ).start()

    def wait_a(s, sem):
        wait_bytes(gathered.at[s, pl.ds(0, n_lat - 1), pl.ds(0, comps)], sem.at[s])

    def send_slots():
        def send(start, dst, kind):
            size = dst.shape[-1]

            @pl.loop(0, n_lon)
            def _(k):
                pltpu.make_async_remote_copy(
                    src_ref=slots.at[0, 0, :, pl.ds(start, size)],
                    dst_ref=dst,
                    send_sem=send_i.at[kind],
                    recv_sem=recv_i.at[kind],
                    device_id=(other, a, k),
                    device_id_type=MESH,
                ).start()

        pl.when(first_a)(lambda: send(0, idx_rows.at[b], 0))
        pl.when(last_a)(lambda: send(2 * cols, idx_rows.at[b], 0))
        pl.when(first_b)(lambda: send(4 * cols, idx_sides.at[0], 1))
        pl.when(last_b)(lambda: send(4 * cols + 2 * rows, idx_sides.at[1], 1))

    def wait_slots():
        pl.when(edge_a)(lambda: wait_bytes(idx_rows, recv_i.at[0]))
        wait_bytes(idx_sides, recv_i.at[1])

    groups = -(-n_lat * n_slots // cols)
    lane8 = lane[0:8]

    def settle(s):
        for level in range(levels):
            totals = [jnp.zeros((8, cols), jnp.float32)] * groups
            for k in range(n_lat):
                low, high = k * n_slots, (k + 1) * n_slots
                turned = pltpu.roll(gathered[s, k], (low - level * half) % cols, 1)
                for g in range(low // cols, (high - 1) // cols + 1):
                    here = jnp.logical_and(lane8 >= low - g * cols, lane8 < high - g * cols)
                    totals[g] = jnp.where(here, turned, totals[g])
            for g in range(groups):
                dense[s, level, g] = totals[g]

    def pick(s, wanted):
        device = ((wanted >> 4) * 21846) >> 16
        row_of = device >> (n_lon.bit_length() - 1)
        number = wanted - (device - row_of) * n_slots
        group = jnp.where(device - row_of * n_lon == b, number >> (cols.bit_length() - 1), -1)
        group = jnp.broadcast_to(group, (8, cols))
        place = jnp.broadcast_to(number & (cols - 1), (8, cols))
        totals = [jnp.zeros((8, cols), jnp.float32)] * levels
        for g in range(groups):
            mine = group == g
            for level in range(levels):
                totals[level] = jnp.where(mine, lane_take(dense[s, level, g], place), totals[level])
        return totals

    def send_parts(s):
        def to(src, dst, kind, k):
            return pltpu.make_async_remote_copy(
                src_ref=src,
                dst_ref=dst.at[s, b, :, :, pl.ds(0, comps)] if kind == 0 else dst.at[s, b, :, pl.ds(0, comps)],
                send_sem=send_b.at[s, kind],
                recv_sem=recv_b.at[s, kind],
                device_id=(other, a, k),
                device_id_type=MESH,
            )

        settle(s)
        for side in range(2):
            for level, total in enumerate(pick(s, idx_sides[side])):
                side_parts[s, side, level] = total
            to(side_parts.at[s, side, :, pl.ds(0, comps)], side_rim, 1, side * (n_lon - 1)).start()

        @pl.when(edge_a)
        def _():
            order = row_order(n_lon)

            @pl.loop(0, len(order))
            def _(group):
                to_whom = [b ^ pick_at(group, way) for way in zip(*order)]
                for k in to_whom:
                    for t in range(2):
                        for level, total in enumerate(
                            pick(s, idx_rows[k, :, t * cols : (t + 1) * cols])
                        ):
                            row_parts[s, k, t, level] = total
                for k in to_whom:
                    to(row_parts.at[s, k, :, :, pl.ds(0, comps)], row_rim, 0, k).start()

    def take_rim(s):
        @pl.when(edge_a)
        def _():
            wait_bytes(row_rim.at[s, :, :, :, pl.ds(0, comps)], recv_b.at[s, 0])
            total = jnp.sum(row_rim[s], axis=0)

            def put(at):
                for t in range(2):
                    for level in range(levels):
                        for c in range(comps):
                            ext[s, c, level, at + t : at + t + 1, :] = total[t, level, c : c + 1, :]

            pl.when(first_a)(lambda: put(PAD - 2))
            pl.when(last_a)(lambda: put(PAD + rows))

        @pl.when(edge_b)
        def _():
            wait_bytes(side_rim.at[s, :, :, pl.ds(0, comps)], recv_b.at[s, 1])
            total = jnp.sum(side_rim[s], axis=0)

            def put(side):
                flip[...] = jnp.zeros_like(flip)
                for level in range(levels):
                    both = (total[level], pltpu.roll(total[level], half, 1))
                    for t in range(2):
                        for c in range(comps):
                            at = 4 * (c * levels + level) + 2 * side + t
                            flip[at : at + 1, :] = both[t][c : c + 1, :]
                pack_from[s, side] = flip[...].T[0:rows, :]

            pl.when(first_b)(lambda: put(0))
            pl.when(last_b)(lambda: put(1))

    def wait_halo(s):
        landed = (rows_from.at[s, 0], rows_from.at[s, 1], pack_from.at[s, 0], pack_from.at[s, 1])
        for side_of, opposite in ((UP, DOWN), (DOWN, UP), (LEFT, RIGHT), (RIGHT, LEFT)):

            @pl.when(neighbours[side_of][0])
            def _():
                wait_bytes(landed[side_of], recv_h.at[s, opposite])
                if side_of in (UP, DOWN):
                    at = PAD - 2 if side_of == UP else PAD + rows
                    for f in range(comps * levels):
                        ext[s, f // levels, f % levels, at : at + 2, :] = rows_from[s, side_of, f]

    def rates(s, emit, low_row=0, count=0):
        chunk = count or rows
        for base in (low_row,):
            lanes = lane[0:chunk]
            beside = jnp.where(
                lanes & 2 == 0,
                pack_from[s, 0, base : base + chunk, :],
                pack_from[s, 1, base : base + chunk, :],
            )

            def at(c, level, shift=0):
                low = PAD + base + shift
                return ext[s, c, level, low : low + chunk, :]

            for level in range(levels):
                u1, u2 = at(1, level) * (1.0 / 12.0), at(2, level) * (1.0 / 12.0)
                b1, b2 = at(4, level) * (1.0 / 12.0), at(5, level) * (1.0 / 12.0)

                def terms(c, with_b):
                    mid = at(c, level)
                    around = pltpu.roll(beside, (cols - 2 - 4 * (c * levels + level)) % cols, 1)
                    west1 = pltpu.roll(jnp.where(lanes == cols - 1, around, mid), 1, 1)
                    west2 = pltpu.roll(jnp.where(lanes >= cols - 2, around, mid), 2, 1)
                    east1 = pltpu.roll(jnp.where(lanes == 0, around, mid), cols - 1, 1)
                    east2 = pltpu.roll(jnp.where(lanes < 2, around, mid), cols - 2, 1)
                    north1, south1 = at(c, level, -1), at(c, level, 1)
                    d_lat = 8.0 * (south1 - north1) - (at(c, level, 2) - at(c, level, -2))
                    d_lon = 8.0 * (east1 - west1) - (east2 - west2)
                    lap = south1 + north1 + east1 + west1 + at(c, 1 - level) - 6.0 * mid
                    adv_u = u1 * d_lat + u2 * d_lon
                    adv_b = b1 * d_lat + b2 * d_lon if with_b else None
                    return mid, adv_u, adv_b, DIFFUSION * lap

                for c in range(3):
                    mid, adv_u, adv_b, lap = terms(c, True)
                    mid_b, adv_ub, adv_bb, lap_b = terms(c + 3, True)
                    moment = adv_bb - adv_u + lap
                    if c == 0:
                        moment = moment + BUOYANCY * at(6, level)
                    emit(c, level, base, mid, moment)
                    emit(c + 3, level, base, mid_b, adv_b - adv_ub + lap_b)
                mid, adv_u, _, lap = terms(6, False)
                emit(6, level, base, mid, lap - adv_u)

    def first_section(c, level, base, mid, rate):
        ext[1, c, level, PAD + base : PAD + base + mid.shape[0], :] = mid + STEP * rate

    def second_section(c, level, base, mid, rate):
        start = ext[0, c, level, PAD + base : PAD + base + mid.shape[0], :]
        out[0, c, level, base : base + mid.shape[0], :] = 0.5 * start + 0.5 * (mid + STEP * rate)

    def give(s):
        donate(s)
        if s == 0:
            pl.semaphore_wait(barrier, greeted)
        start_a(s)
        if s == 0:
            send_slots()
        pack_sides(s)
        pack_rows(s)
        start_halo(s)

    def mend_side(s):
        rim = jnp.where(first_b, pack_from[s, 0], pack_from[s, 1])
        spot = lane & 3
        near_w, far_w = pltpu.roll(rim, 1, 1), pltpu.roll(rim, 2, 1)
        near_e, far_e = pltpu.roll(rim, cols - 1, 1), pltpu.roll(rim, cols - 2, 1)
        slope = jnp.where(
            spot == 2,
            far_w - 8.0 * near_w,
            jnp.where(spot == 3, far_w, jnp.where(spot == 1, 8.0 * near_e - far_e, -far_e)),
        ) * (1.0 / 12.0)
        lap = jnp.where(spot == 2, near_w, jnp.where(spot == 1, near_e, 0.0))
        per_comp = 4 * levels
        within = lane & (per_comp - 1)
        u2 = lane_take(pack[s], within + 2 * per_comp)
        b2 = lane_take(pack[s], within + 5 * per_comp)
        swap = 3 * per_comp
        partner = jnp.where(
            lane < swap,
            pltpu.roll(slope, cols - swap, 1),
            jnp.where(lane < 2 * swap, pltpu.roll(slope, swap, 1), 0.0),
        )
        scale = STEP if s == 0 else 0.5 * STEP
        change = scale * (DIFFUSION * lap - u2 * slope + b2 * partner)
        outer = jnp.logical_or(lane >= cols - 2, lane < 2)
        for f in range(comps * levels):
            c, level = f // levels, f % levels
            here = jnp.where(outer, pltpu.roll(change, (cols - 2 - 4 * f) % cols, 1), 0.0)
            if s == 0:
                ext[1, c, level, PAD : PAD + rows, :] = inner(1, c, level) + here
            else:
                out[0, c, level] = out[0, c, level] + here

    def mend(s, emit):
        take_rim(s)
        pl.when(edge_b)(lambda: mend_side(s))
        pl.when(first_a)(lambda: rates(s, emit, 0, 8))
        pl.when(last_a)(lambda: rates(s, emit, rows - 8, 8))

    for s in range(2):

        @pl.when(first_b)
        def _():
            pack_from[s, 0] = jnp.zeros((rows, cols), jnp.float32)

        @pl.when(last_b)
        def _():
            pack_from[s, 1] = jnp.zeros((rows, cols), jnp.float32)

    loads[3].wait()
    give(0)
    wait_halo(0)
    rates(0, first_section)
    wait_a(0, recv_a)
    wait_slots()
    send_parts(0)

    pl.when(edge)(lambda: mend(0, first_section))
    give(1)

    wait_a(1, recv_a)
    send_parts(1)
    wait_halo(1)
    rates(1, second_section)
    for s in range(2):
        wait_a(s, send_a)
        for (there, _), copy in zip(neighbours, halo_copies(s)):
            pl.when(there)(copy.wait_send)
    pl.when(edge_a)(lambda: wait_bytes(idx_rows, send_i.at[0]))
    pl.when(edge_b)(lambda: wait_bytes(idx_rows.at[pl.ds(0, n_lon // 2)], send_i.at[1]))

    pl.when(edge)(lambda: mend(1, second_section))

    for s in range(2):
        wait_bytes(side_parts.at[s, :, :, pl.ds(0, comps)], send_b.at[s, 1])
        pl.when(edge_a)(
            functools.partial(wait_bytes, row_parts.at[s, :, :, :, pl.ds(0, comps)], send_b.at[s, 0])
        )


def solution(mesh):
    n_lat, n_lon = mesh.shape["lat"], mesh.shape["lon"]

    def per_device(state, source_slot, donor_cell, donor_frac, donor_turn):
        _, comps, levels, rows, cols = state.shape
        f32, i32, dma = jnp.float32, jnp.int32, pltpu.SemaphoreType.DMA
        vmem = pl.BlockSpec(memory_space=pltpu.VMEM)
        return pl.pallas_call(
            functools.partial(kernel, n_lat, n_lon),
            out_shape=jax.ShapeDtypeStruct(state.shape, f32),
            in_specs=[pl.BlockSpec(memory_space=pltpu.HBM)] * 5,
            out_specs=vmem,
            scratch_shapes=[
                pltpu.VMEM((2, comps, levels, rows + 2 * PAD, cols), f32),
                pltpu.VMEM((1, donor_cell.shape[3]), i32),
                pltpu.VMEM((1, donor_cell.shape[3]), f32),
                pltpu.VMEM((2, donor_cell.shape[3]), f32),
                pltpu.VMEM((8, cols), i32),
                pltpu.VMEM((8, cols), f32),
                pltpu.VMEM((2, 2, comps * levels, 2, cols), f32),
                pltpu.VMEM((2, 2, comps * levels, 2, cols), f32),
                pltpu.VMEM((2, rows, cols), f32),
                pltpu.VMEM((2, 2, rows, cols), f32),
                pltpu.VMEM((2, n_lat, 8, cols), f32),
                pltpu.VMEM((2, levels, -(-n_lat * donor_cell.shape[3] // cols), 8, cols), f32),
                pltpu.VMEM((n_lon, 1, 2 * cols), i32),
                pltpu.VMEM((2, 1, 2 * rows), i32),
                pltpu.VMEM((2, n_lon, 2, levels, 8, cols), f32),
                pltpu.VMEM((2, 2, levels, 8, cols), f32),
                pltpu.VMEM((2, n_lon, 2, levels, 8, cols), f32),
                pltpu.VMEM((2, n_lon, levels, 8, cols), f32),
                pltpu.VMEM((cols, cols), f32),
                dma((4,)),
                dma((2,)),
                dma((2,)),
                dma((2, 4)),
                dma((2, 4)),
                dma((2,)),
                dma((2,)),
                dma((2, 2)),
                dma((2, 2)),
            ],
            compiler_params=pltpu.CompilerParams(
                collective_id=0, has_side_effects=True, vmem_limit_bytes=32 * 2**20
            ),
        )(
            *(
                pltpu.with_memory_space_constraint(x, pltpu.HBM)
                for x in (state, source_slot, donor_cell, donor_frac, donor_turn)
            )
        )

    in_specs = (
        P("panel", None, None, "lat", "lon"),
        P("panel", "lat", "lon", None),
        P("panel", "lat", "lon", None),
        P("panel", "lat", "lon", None, None),
        P("panel", "lat", "lon", None),
    )
    out_specs = P("panel", None, None, "lat", "lon")
    return jax.shard_map(
        per_device, mesh=mesh, in_specs=in_specs, out_specs=out_specs, check_vma=False
    )
```

```python
import functools

import jax
import jax.numpy as jnp
from jax import lax
from jax.experimental import pallas as pl
from jax.experimental.pallas import tpu as pltpu
from jax.sharding import PartitionSpec as P

MESH = pl.DeviceIdType.MESH
DIFFUSION = 0.05
BUOYANCY = 0.5
STEP = 0.25
PAD = 8
UP, DOWN, LEFT, RIGHT = range(4)


def row_order(n_lon):
    ways = sorted(range(n_lon), key=lambda d: -(2 if d & 6 == 4 else 1 if d & 6 else 0))
    size = min(4, n_lon // 2)
    return [ways[i : i + size] for i in range(0, n_lon, size)]


def pick_at(index, values):
    result = values[-1]
    for i, value in enumerate(values[:-1]):
        result = jnp.where(index == i, value, result)
    return result


def lane_take(value, index):
    return jnp.take_along_axis(value, index, axis=1, mode="promise_in_bounds")


def kernel(
    n_lat, n_lon, state, slots, cell, frac, turn, out,
    ext, cell_at, turn_at, frac_at, whole_i, whole_f, rows_to, rows_from, pack, pack_from, gathered, dense, idx_rows, idx_sides,
    row_parts, side_parts, row_rim, side_rim, flip, helped, dense_x, row_parts_x,
    load_sem, send_a, recv_a, send_h, recv_h, send_i, recv_i, send_b, recv_b, send_x, recv_x, send_y,
):
    comps, levels, rows, cols = state.shape[1:]
    n_slots = cell.shape[3]
    half = cols // 2
    p = lax.axis_index("panel")
    a = lax.axis_index("lat")
    b = lax.axis_index("lon")
    other = 1 - p
    first_a, last_a = a == 0, a == n_lat - 1
    first_b, last_b = b == 0, b == n_lon - 1
    edge_a = jnp.logical_or(first_a, last_a)
    edge_b = jnp.logical_or(first_b, last_b)
    edge = jnp.logical_or(edge_a, edge_b)
    twin = b ^ 1
    helps = jnp.logical_and(edge_a, jnp.logical_or(twin == 0, twin == n_lon - 1))

    neighbours = (
        (a > 0, (p, a - 1, b)),
        (a < n_lat - 1, (p, a + 1, b)),
        (b > 0, (p, a, b - 1)),
        (b < n_lon - 1, (p, a, b + 1)),
    )

    loads = [
        pltpu.make_async_copy(cell.at[0, 0], cell_at, load_sem.at[1]),
        pltpu.make_async_copy(turn.at[0, 0], turn_at, load_sem.at[2]),
        pltpu.make_async_copy(frac.at[0, 0, 0], frac_at, load_sem.at[3]),
        pltpu.make_async_copy(
            state.at[0], ext.at[0, :, :, pl.ds(PAD, rows), :], load_sem.at[0]
        ),
    ]
    for load in loads:
        load.start()

    def far_first(k):
        step = (k + 1) >> 1
        return n_lat // 2 + jnp.where(k & 1 == 1, step, -step)

    barrier = pltpu.get_barrier_semaphore()

    def greet(device):
        pl.semaphore_signal(barrier, inc=1, device_id=device, device_id_type=MESH)

    @pl.loop(0, n_lat - 1)
    def _(k):
        greet((p, lax.rem(a + far_first(k), n_lat), b))

    @pl.loop(0, n_lon)
    def _(k):
        greet((other, a, k))

    @pl.when(helps)
    def _():
        @pl.loop(0, n_lat)
        def _(k):
            greet((p, k, twin))

    for there, device in neighbours[2:]:
        pl.when(there)(functools.partial(greet, device))
    greeted = n_lon + n_lat - 1 + (b > 0).astype(jnp.int32) + (b < n_lon - 1).astype(jnp.int32)
    greeted = greeted + jnp.where(edge_b, 2, 0)

    for load in loads[:3]:
        load.wait()
    whole_i[...] = jnp.zeros_like(whole_i)
    whole_f[...] = jnp.zeros_like(whole_f)
    for start in (0, half):
        whole_i[0:1, start : start + n_slots] = cell_at[...]
        whole_f[0:1, start : start + n_slots] = turn_at[...]
        whole_f[1:3, start : start + n_slots] = frac_at[...]
    cells = whole_i[0:1, :]
    turns = whole_f[0:1, :]
    cosine = jnp.cos(turns)
    sine = jnp.sin(turns)
    frac_t = whole_f[1:2, :]
    frac_p = whole_f[2:3, :]
    row = (cells * 33027) >> 22
    col = cells - row * (cols - 1)
    row_at = lax.broadcasted_iota(jnp.int32, (rows, cols), 0)
    row_full = jnp.broadcast_to(row, (rows, cols))
    weight_t = jnp.where(
        row_at == row_full,
        jnp.broadcast_to(1.0 - frac_t, (rows, cols)),
        jnp.where(row_at == row_full + 1, jnp.broadcast_to(frac_t, (rows, cols)), 0.0),
    )
    lane = lax.broadcasted_iota(jnp.int32, (rows, cols), 1)
    low_lane = lane < half
    col_at = jnp.broadcast_to(col, (rows, cols)) + jnp.where(low_lane, 0, 1)
    weight = weight_t * jnp.where(
        low_lane,
        jnp.broadcast_to(1.0 - frac_p, (rows, cols)),
        jnp.broadcast_to(frac_p, (rows, cols)),
    )

    def inner(s, c, level, shift=0):
        return ext[s, c, level, PAD + shift : PAD + shift + rows, :]

    def donate(s):
        given = []
        for c in range(comps):
            sums = []
            for level in range(levels):
                halves = jnp.sum(lane_take(inner(s, c, level), col_at) * weight, axis=0, keepdims=True)
                sums.append(halves + pltpu.roll(halves, half, 1))
            given.append(jnp.where(low_lane[0:1], sums[0], sums[1]))
        for i in (1, 4):
            x, y = given[i], given[i + 1]
            given[i], given[i + 1] = cosine * x - sine * y, sine * x + cosine * y
        for c in range(comps):
            gathered[s, a, c : c + 1, :] = given[c]

    def pack_sides(s):
        packed = jnp.zeros((rows, cols), jnp.float32)
        for f in range(comps * levels):
            turned = pltpu.roll(inner(s, f // levels, f % levels), 4 * f + 2, 1)
            packed = jnp.where(lane >> 2 == f, turned, packed)
        pack[s] = packed

    def pack_rows(s):
        for f in range(comps * levels):
            c, level = f // levels, f % levels
            rows_to[s, 0, f] = ext[s, c, level, PAD : PAD + 2, :]
            rows_to[s, 1, f] = ext[s, c, level, PAD + rows - 2 : PAD + rows, :]

    def halo_copies(s):
        pairs = (
            (rows_to.at[s, 0], rows_from.at[s, 1]),
            (rows_to.at[s, 1], rows_from.at[s, 0]),
            (pack.at[s], pack_from.at[s, 1]),
            (pack.at[s], pack_from.at[s, 0]),
        )
        copies = []
        for to, (src, dst) in enumerate(pairs):
            copies.append(
                pltpu.make_async_remote_copy(
                    src_ref=src,
                    dst_ref=dst,
                    send_sem=send_h.at[s, to],
                    recv_sem=recv_h.at[s, to],
                    device_id=neighbours[to][1],
                    device_id_type=MESH,
                )
            )
        return copies

    def wait_bytes(ref, sem):
        pltpu.make_async_copy(ref, ref, sem).wait()

    def start_halo(s):
        for (there, _), copy in zip(neighbours, halo_copies(s)):
            pl.when(there)(copy.start)

    def start_a(s):
        @pl.loop(0, n_lat - 1)
        def _(i):
            k = i if s == 0 else jnp.where(edge_a, n_lat - 2 - i, i)
            pltpu.make_async_remote_copy(
                src_ref=gathered.at[s, a, pl.ds(0, comps)],
                dst_ref=gathered.at[s, a, pl.ds(0, comps)],
                send_sem=send_a.at[s],
                recv_sem=recv_a.at[s],
                device_id=(p, lax.rem(a + far_first(k), n_lat), b),
                device_id_type=MESH,
            ).start()

    def help_copy(i):
        return pltpu.make_async_remote_copy(
            src_ref=gathered.at[1, a, pl.ds(0, comps)],
            dst_ref=helped.at[a, pl.ds(0, comps)],
            send_sem=send_x.at[i],
            recv_sem=recv_x,
            device_id=(p, i * (n_lat - 1), twin),
            device_id_type=MESH,
        )

    def wait_a(s, sem):
        wait_bytes(gathered.at[s, pl.ds(0, n_lat - 1), pl.ds(0, comps)], sem.at[s])

    def send_slots():
        def send(start, dst, kind):
            size = dst.shape[-1]

            @pl.loop(0, n_lon)
            def _(k):
                pltpu.make_async_remote_copy(
                    src_ref=slots.at[0, 0, :, pl.ds(start, size)],
                    dst_ref=dst,
                    send_sem=send_i.at[kind],
                    recv_sem=recv_i.at[kind],
                    device_id=(other, a, k),
                    device_id_type=MESH,
                ).start()

        pl.when(first_a)(lambda: send(0, idx_rows.at[b], 0))
        pl.when(last_a)(lambda: send(2 * cols, idx_rows.at[b], 0))
        pl.when(first_b)(lambda: send(4 * cols, idx_sides.at[0], 1))
        pl.when(last_b)(lambda: send(4 * cols + 2 * rows, idx_sides.at[1], 1))

    def wait_slots():
        pl.when(edge_a)(lambda: wait_bytes(idx_rows, recv_i.at[0]))
        wait_bytes(idx_sides, recv_i.at[1])

    groups = -(-n_lat * n_slots // cols)
    lane8 = lane[0:8]

    def settle(block_of, packed):
        for level in range(levels):
            totals = [jnp.zeros((8, cols), jnp.float32)] * groups
            for k in range(n_lat):
                low, high = k * n_slots, (k + 1) * n_slots
                turned = pltpu.roll(block_of[k], (low - level * half) % cols, 1)
                for g in range(low // cols, (high - 1) // cols + 1):
                    here = jnp.logical_and(lane8 >= low - g * cols, lane8 < high - g * cols)
                    totals[g] = jnp.where(here, turned, totals[g])
            for g in range(groups):
                packed[level, g] = totals[g]

    def pick(packed, column, wanted):
        device = ((wanted >> 4) * 21846) >> 16
        row_of = device >> (n_lon.bit_length() - 1)
        number = wanted - (device - row_of) * n_slots
        group = jnp.where(device - row_of * n_lon == column, number >> (cols.bit_length() - 1), -1)
        group = jnp.broadcast_to(group, (8, cols))
        place = jnp.broadcast_to(number & (cols - 1), (8, cols))
        totals = [jnp.zeros((8, cols), jnp.float32)] * levels
        for g in range(groups):
            mine = group == g
            for level in range(levels):
                totals[level] = jnp.where(mine, lane_take(packed[level, g], place), totals[level])
        return totals

    order = row_order(n_lon)
    late = len(order) // 2

    def part_copy(s, src, dst, sem, kind, k):
        return pltpu.make_async_remote_copy(
            src_ref=src,
            dst_ref=dst,
            send_sem=sem,
            recv_sem=recv_b.at[s, kind],
            device_id=(other, a, k),
            device_id_type=MESH,
        )

    def send_rows(s, packed, column, held, sem, first, last):
        @pl.loop(first, last)
        def _(group):
            to_whom = [column ^ pick_at(group, way) for way in zip(*order)]
            for k in to_whom:
                for t in range(2):
                    wanted = idx_rows[k, :, t * cols : (t + 1) * cols]
                    for level, total in enumerate(pick(packed, column, wanted)):
                        held[k, t, level] = total
            for k in to_whom:
                src = held.at[k, :, :, pl.ds(0, comps)]
                dst = row_rim.at[s, column, :, :, pl.ds(0, comps)]
                part_copy(s, src, dst, sem, 0, k).start()

    def send_parts(s):
        settle(gathered.at[s], dense.at[s])
        for side in range(2):
            for level, total in enumerate(pick(dense.at[s], b, idx_sides[side])):
                side_parts[s, side, level] = total
            src = side_parts.at[s, side, :, pl.ds(0, comps)]
            dst = side_rim.at[s, b, :, pl.ds(0, comps)]
            part_copy(s, src, dst, send_b.at[s, 1], 1, side * (n_lon - 1)).start()

        @pl.when(edge_a)
        def _():
            last = len(order) if s == 0 else jnp.where(edge_b, late, len(order))
            send_rows(s, dense.at[s], b, row_parts.at[s], send_b.at[s, 0], 0, last)

    def help_out():
        wait_bytes(helped.at[:, pl.ds(0, comps)], recv_x)
        settle(helped, dense_x)
        send_rows(1, dense_x, twin, row_parts_x, send_y, late, len(order))

    def take_rim(s):
        @pl.when(edge_a)
        def _():
            wait_bytes(row_rim.at[s, :, :, :, pl.ds(0, comps)], recv_b.at[s, 0])
            total = jnp.sum(row_rim[s], axis=0)

            def put(at):
                for t in range(2):
                    for level in range(levels):
                        for c in range(comps):
                            ext[s, c, level, at + t : at + t + 1, :] = total[t, level, c : c + 1, :]

            pl.when(first_a)(lambda: put(PAD - 2))
            pl.when(last_a)(lambda: put(PAD + rows))

        @pl.when(edge_b)
        def _():
            wait_bytes(side_rim.at[s, :, :, pl.ds(0, comps)], recv_b.at[s, 1])
            total = jnp.sum(side_rim[s], axis=0)

            def put(side):
                flip[...] = jnp.zeros_like(flip)
                for level in range(levels):
                    both = (total[level], pltpu.roll(total[level], half, 1))
                    for t in range(2):
                        for c in range(comps):
                            at = 4 * (c * levels + level) + 2 * side + t
                            flip[at : at + 1, :] = both[t][c : c + 1, :]
                pack_from[s, side] = flip[...].T[0:rows, :]

            pl.when(first_b)(lambda: put(0))
            pl.when(last_b)(lambda: put(1))

    def wait_halo(s):
        landed = (rows_from.at[s, 0], rows_from.at[s, 1], pack_from.at[s, 0], pack_from.at[s, 1])
        for side_of, opposite in ((UP, DOWN), (DOWN, UP), (LEFT, RIGHT), (RIGHT, LEFT)):

            @pl.when(neighbours[side_of][0])
            def _():
                wait_bytes(landed[side_of], recv_h.at[s, opposite])
                if side_of in (UP, DOWN):
                    at = PAD - 2 if side_of == UP else PAD + rows
                    for f in range(comps * levels):
                        ext[s, f // levels, f % levels, at : at + 2, :] = rows_from[s, side_of, f]

    def rates(s, emit, low_row=0, count=0):
        chunk = count or rows
        for base in (low_row,):
            lanes = lane[0:chunk]
            beside = jnp.where(
                lanes & 2 == 0,
                pack_from[s, 0, base : base + chunk, :],
                pack_from[s, 1, base : base + chunk, :],
            )

            def at(c, level, shift=0):
                low = PAD + base + shift
                return ext[s, c, level, low : low + chunk, :]

            for level in range(levels):
                u1, u2 = at(1, level) * (1.0 / 12.0), at(2, level) * (1.0 / 12.0)
                b1, b2 = at(4, level) * (1.0 / 12.0), at(5, level) * (1.0 / 12.0)

                def terms(c, with_b):
                    mid = at(c, level)
                    around = pltpu.roll(beside, (cols - 2 - 4 * (c * levels + level)) % cols, 1)
                    west1 = pltpu.roll(jnp.where(lanes == cols - 1, around, mid), 1, 1)
                    west2 = pltpu.roll(jnp.where(lanes >= cols - 2, around, mid), 2, 1)
                    east1 = pltpu.roll(jnp.where(lanes == 0, around, mid), cols - 1, 1)
                    east2 = pltpu.roll(jnp.where(lanes < 2, around, mid), cols - 2, 1)
                    north1, south1 = at(c, level, -1), at(c, level, 1)
                    d_lat = 8.0 * (south1 - north1) - (at(c, level, 2) - at(c, level, -2))
                    d_lon = 8.0 * (east1 - west1) - (east2 - west2)
                    lap = south1 + north1 + east1 + west1 + at(c, 1 - level) - 6.0 * mid
                    adv_u = u1 * d_lat + u2 * d_lon
                    adv_b = b1 * d_lat + b2 * d_lon if with_b else None
                    return mid, adv_u, adv_b, DIFFUSION * lap

                for c in range(3):
                    mid, adv_u, adv_b, lap = terms(c, True)
                    mid_b, adv_ub, adv_bb, lap_b = terms(c + 3, True)
                    moment = adv_bb - adv_u + lap
                    if c == 0:
                        moment = moment + BUOYANCY * at(6, level)
                    emit(c, level, base, mid, moment)
                    emit(c + 3, level, base, mid_b, adv_b - adv_ub + lap_b)
                mid, adv_u, _, lap = terms(6, False)
                emit(6, level, base, mid, lap - adv_u)

    def first_section(c, level, base, mid, rate):
        ext[1, c, level, PAD + base : PAD + base + mid.shape[0], :] = mid + STEP * rate

    def second_section(c, level, base, mid, rate):
        start = ext[0, c, level, PAD + base : PAD + base + mid.shape[0], :]
        out[0, c, level, base : base + mid.shape[0], :] = 0.5 * start + 0.5 * (mid + STEP * rate)

    def give(s):
        donate(s)
        if s == 0:
            pl.semaphore_wait(barrier, greeted)
        if s == 1:
            for i in range(2):
                pl.when(edge_b)(help_copy(i).start)
        start_a(s)
        if s == 0:
            send_slots()
        pack_sides(s)
        pack_rows(s)
        start_halo(s)

    def mend_side(s):
        rim = jnp.where(first_b, pack_from[s, 0], pack_from[s, 1])
        spot = lane & 3
        near_w, far_w = pltpu.roll(rim, 1, 1), pltpu.roll(rim, 2, 1)
        near_e, far_e = pltpu.roll(rim, cols - 1, 1), pltpu.roll(rim, cols - 2, 1)
        slope = jnp.where(
            spot == 2,
            far_w - 8.0 * near_w,
            jnp.where(spot == 3, far_w, jnp.where(spot == 1, 8.0 * near_e - far_e, -far_e)),
        ) * (1.0 / 12.0)
        lap = jnp.where(spot == 2, near_w, jnp.where(spot == 1, near_e, 0.0))
        per_comp = 4 * levels
        within = lane & (per_comp - 1)
        u2 = lane_take(pack[s], within + 2 * per_comp)
        b2 = lane_take(pack[s], within + 5 * per_comp)
        swap = 3 * per_comp
        partner = jnp.where(
            lane < swap,
            pltpu.roll(slope, cols - swap, 1),
            jnp.where(lane < 2 * swap, pltpu.roll(slope, swap, 1), 0.0),
        )
        scale = STEP if s == 0 else 0.5 * STEP
        change = scale * (DIFFUSION * lap - u2 * slope + b2 * partner)
        outer = jnp.logical_or(lane >= cols - 2, lane < 2)
        for f in range(comps * levels):
            c, level = f // levels, f % levels
            here = jnp.where(outer, pltpu.roll(change, (cols - 2 - 4 * f) % cols, 1), 0.0)
            if s == 0:
                ext[1, c, level, PAD : PAD + rows, :] = inner(1, c, level) + here
            else:
                out[0, c, level] = out[0, c, level] + here

    def mend(s, emit):
        take_rim(s)
        pl.when(edge_b)(lambda: mend_side(s))
        pl.when(first_a)(lambda: rates(s, emit, 0, 8))
        pl.when(last_a)(lambda: rates(s, emit, rows - 8, 8))

    for s in range(2):

        @pl.when(first_b)
        def _():
            pack_from[s, 0] = jnp.zeros((rows, cols), jnp.float32)

        @pl.when(last_b)
        def _():
            pack_from[s, 1] = jnp.zeros((rows, cols), jnp.float32)

    loads[3].wait()
    give(0)
    wait_halo(0)
    rates(0, first_section)
    wait_a(0, recv_a)
    wait_slots()
    send_parts(0)

    pl.when(edge)(lambda: mend(0, first_section))
    give(1)

    wait_a(1, recv_a)
    send_parts(1)
    wait_halo(1)
    rates(1, second_section)
    pl.when(helps)(help_out)
    for s in range(2):
        wait_a(s, send_a)
        for (there, _), copy in zip(neighbours, halo_copies(s)):
            pl.when(there)(copy.wait_send)
    pl.when(edge_a)(lambda: wait_bytes(idx_rows, send_i.at[0]))
    pl.when(edge_b)(lambda: wait_bytes(idx_rows.at[pl.ds(0, n_lon // 2)], send_i.at[1]))

    pl.when(edge)(lambda: mend(1, second_section))

    for s in range(2):
        wait_bytes(side_parts.at[s, :, :, pl.ds(0, comps)], send_b.at[s, 1])
    shared = n_lon * late // len(order)
    sent = [row_parts.at[s, :, :, :, pl.ds(0, comps)] for s in range(2)]
    half_sent = row_parts.at[1, pl.ds(0, shared), :, :, pl.ds(0, comps)]
    rest_sent = row_parts_x.at[pl.ds(0, n_lon - shared), :, :, pl.ds(0, comps)]
    pl.when(edge_a)(lambda: wait_bytes(sent[0], send_b.at[0, 0]))
    inside = jnp.logical_and(edge_a, jnp.logical_not(edge_b))
    pl.when(inside)(lambda: wait_bytes(sent[1], send_b.at[1, 0]))
    pl.when(jnp.logical_and(edge_a, edge_b))(lambda: wait_bytes(half_sent, send_b.at[1, 0]))
    pl.when(helps)(lambda: wait_bytes(rest_sent, send_y))
    for i in range(2):
        pl.when(edge_b)(help_copy(i).wait_send)


def solution(mesh):
    n_lat, n_lon = mesh.shape["lat"], mesh.shape["lon"]

    def per_device(state, source_slot, donor_cell, donor_frac, donor_turn):
        _, comps, levels, rows, cols = state.shape
        f32, i32, dma = jnp.float32, jnp.int32, pltpu.SemaphoreType.DMA
        vmem = pl.BlockSpec(memory_space=pltpu.VMEM)
        return pl.pallas_call(
            functools.partial(kernel, n_lat, n_lon),
            out_shape=jax.ShapeDtypeStruct(state.shape, f32),
            in_specs=[pl.BlockSpec(memory_space=pltpu.HBM)] * 5,
            out_specs=vmem,
            scratch_shapes=[
                pltpu.VMEM((2, comps, levels, rows + 2 * PAD, cols), f32),
                pltpu.VMEM((1, donor_cell.shape[3]), i32),
                pltpu.VMEM((1, donor_cell.shape[3]), f32),
                pltpu.VMEM((2, donor_cell.shape[3]), f32),
                pltpu.VMEM((8, cols), i32),
                pltpu.VMEM((8, cols), f32),
                pltpu.VMEM((2, 2, comps * levels, 2, cols), f32),
                pltpu.VMEM((2, 2, comps * levels, 2, cols), f32),
                pltpu.VMEM((2, rows, cols), f32),
                pltpu.VMEM((2, 2, rows, cols), f32),
                pltpu.VMEM((2, n_lat, 8, cols), f32),
                pltpu.VMEM((2, levels, -(-n_lat * donor_cell.shape[3] // cols), 8, cols), f32),
                pltpu.VMEM((n_lon, 1, 2 * cols), i32),
                pltpu.VMEM((2, 1, 2 * rows), i32),
                pltpu.VMEM((2, n_lon, 2, levels, 8, cols), f32),
                pltpu.VMEM((2, 2, levels, 8, cols), f32),
                pltpu.VMEM((2, n_lon, 2, levels, 8, cols), f32),
                pltpu.VMEM((2, n_lon, levels, 8, cols), f32),
                pltpu.VMEM((cols, cols), f32),
                pltpu.VMEM((n_lat, 8, cols), f32),
                pltpu.VMEM((levels, -(-n_lat * donor_cell.shape[3] // cols), 8, cols), f32),
                pltpu.VMEM((n_lon, 2, levels, 8, cols), f32),
                dma((4,)),
                dma((2,)),
                dma((2,)),
                dma((2, 4)),
                dma((2, 4)),
                dma((2,)),
                dma((2,)),
                dma((2, 2)),
                dma((2, 2)),
                dma((2,)),
                dma,
                dma,
            ],
            compiler_params=pltpu.CompilerParams(
                collective_id=0, has_side_effects=True, vmem_limit_bytes=32 * 2**20
            ),
        )(
            *(
                pltpu.with_memory_space_constraint(x, pltpu.HBM)
                for x in (state, source_slot, donor_cell, donor_frac, donor_turn)
            )
        )

    in_specs = (
        P("panel", None, None, "lat", "lon"),
        P("panel", "lat", "lon", None),
        P("panel", "lat", "lon", None),
        P("panel", "lat", "lon", None, None),
        P("panel", "lat", "lon", None),
    )
    out_specs = P("panel", None, None, "lat", "lon")
    return jax.shard_map(
        per_device, mesh=mesh, in_specs=in_specs, out_specs=out_specs, check_vma=False
    )
```

```python
import functools

import jax
import jax.numpy as jnp
from jax import lax
from jax.experimental import pallas as pl
from jax.experimental.pallas import tpu as pltpu
from jax.sharding import PartitionSpec as P

MESH = pl.DeviceIdType.MESH
DIFFUSION = 0.05
BUOYANCY = 0.5
STEP = 0.25
PAD = 8
UP, DOWN, LEFT, RIGHT = range(4)


def row_order(n_lon):
    ways = sorted(range(n_lon), key=lambda d: -(2 if d & 6 == 4 else 1 if d & 6 else 0))
    size = min(4, n_lon // 2)
    return [ways[i : i + size] for i in range(0, n_lon, size)]


def pick_at(index, values):
    result = values[-1]
    for i, value in enumerate(values[:-1]):
        result = jnp.where(index == i, value, result)
    return result


def lane_take(value, index):
    return jnp.take_along_axis(value, index, axis=1, mode="promise_in_bounds")


def kernel(
    n_lat, n_lon, state, slots, cell, frac, turn, out,
    ext, cell_at, turn_at, frac_at, whole_i, whole_f, rows_to, rows_from, pack, pack_from, gathered, dense, idx_rows, idx_sides,
    row_parts, side_parts, row_rim, side_rim, flip, helped, dense_x, row_parts_x,
    load_sem, send_a, recv_a, send_h, recv_h, send_i, recv_i, send_b, recv_b, send_x, recv_x, send_y,
):
    comps, levels, rows, cols = state.shape[1:]
    n_slots = cell.shape[3]
    half = cols // 2
    p = lax.axis_index("panel")
    a = lax.axis_index("lat")
    b = lax.axis_index("lon")
    other = 1 - p
    first_a, last_a = a == 0, a == n_lat - 1
    first_b, last_b = b == 0, b == n_lon - 1
    edge_a = jnp.logical_or(first_a, last_a)
    edge_b = jnp.logical_or(first_b, last_b)
    edge = jnp.logical_or(edge_a, edge_b)
    twin = b ^ 1
    helps = jnp.logical_and(edge_a, jnp.logical_or(twin == 0, twin == n_lon - 1))

    neighbours = (
        (a > 0, (p, a - 1, b)),
        (a < n_lat - 1, (p, a + 1, b)),
        (b > 0, (p, a, b - 1)),
        (b < n_lon - 1, (p, a, b + 1)),
    )

    loads = [
        pltpu.make_async_copy(cell.at[0, 0], cell_at, load_sem.at[1]),
        pltpu.make_async_copy(turn.at[0, 0], turn_at, load_sem.at[2]),
        pltpu.make_async_copy(frac.at[0, 0, 0], frac_at, load_sem.at[3]),
        pltpu.make_async_copy(
            state.at[0], ext.at[0, :, :, pl.ds(PAD, rows), :], load_sem.at[0]
        ),
    ]
    for load in loads:
        load.start()

    def far_first(k):
        step = (k + 1) >> 1
        return n_lat // 2 + jnp.where(k & 1 == 1, step, -step)

    barrier = pltpu.get_barrier_semaphore()

    def greet(device):
        pl.semaphore_signal(barrier, inc=1, device_id=device, device_id_type=MESH)

    @pl.loop(0, n_lat - 1)
    def _(k):
        greet((p, lax.rem(a + far_first(k), n_lat), b))

    @pl.loop(0, n_lon)
    def _(k):
        greet((other, a, k))

    @pl.when(helps)
    def _():
        @pl.loop(0, n_lat)
        def _(k):
            greet((p, k, twin))

    for there, device in neighbours[2:]:
        pl.when(there)(functools.partial(greet, device))
    greeted = n_lon + n_lat - 1 + (b > 0).astype(jnp.int32) + (b < n_lon - 1).astype(jnp.int32)
    greeted = greeted + jnp.where(edge_b, 2, 0)

    for load in loads[:3]:
        load.wait()
    whole_i[...] = jnp.zeros_like(whole_i)
    whole_f[...] = jnp.zeros_like(whole_f)
    for start in (0, half):
        whole_i[0:1, start : start + n_slots] = cell_at[...]
        whole_f[0:1, start : start + n_slots] = turn_at[...]
        whole_f[1:3, start : start + n_slots] = frac_at[...]
    cells = whole_i[0:1, :]
    turns = whole_f[0:1, :]
    cosine = jnp.cos(turns)
    sine = jnp.sin(turns)
    frac_t = whole_f[1:2, :]
    frac_p = whole_f[2:3, :]
    row = (cells * 33027) >> 22
    col = cells - row * (cols - 1)
    row_at = lax.broadcasted_iota(jnp.int32, (rows, cols), 0)
    row_full = jnp.broadcast_to(row, (rows, cols))
    weight_t = jnp.where(
        row_at == row_full,
        jnp.broadcast_to(1.0 - frac_t, (rows, cols)),
        jnp.where(row_at == row_full + 1, jnp.broadcast_to(frac_t, (rows, cols)), 0.0),
    )
    lane = lax.broadcasted_iota(jnp.int32, (rows, cols), 1)
    low_lane = lane < half
    col_at = jnp.broadcast_to(col, (rows, cols)) + jnp.where(low_lane, 0, 1)
    weight = weight_t * jnp.where(
        low_lane,
        jnp.broadcast_to(1.0 - frac_p, (rows, cols)),
        jnp.broadcast_to(frac_p, (rows, cols)),
    )

    def inner(s, c, level, shift=0):
        return ext[s, c, level, PAD + shift : PAD + shift + rows, :]

    def donate(s):
        given = []
        for c in range(comps):
            sums = []
            for level in range(levels):
                halves = jnp.sum(lane_take(inner(s, c, level), col_at) * weight, axis=0, keepdims=True)
                sums.append(halves + pltpu.roll(halves, half, 1))
            given.append(jnp.where(low_lane[0:1], sums[0], sums[1]))
        for i in (1, 4):
            x, y = given[i], given[i + 1]
            given[i], given[i + 1] = cosine * x - sine * y, sine * x + cosine * y
        for c in range(comps):
            gathered[s, a, c : c + 1, :] = given[c]

    def pack_sides(s):
        packed = jnp.zeros((rows, cols), jnp.float32)
        for f in range(comps * levels):
            turned = pltpu.roll(inner(s, f // levels, f % levels), 4 * f + 2, 1)
            packed = jnp.where(lane >> 2 == f, turned, packed)
        pack[s] = packed

    def pack_rows(s):
        for f in range(comps * levels):
            c, level = f // levels, f % levels
            rows_to[s, 0, f] = ext[s, c, level, PAD : PAD + 2, :]
            rows_to[s, 1, f] = ext[s, c, level, PAD + rows - 2 : PAD + rows, :]

    def halo_copies(s):
        pairs = (
            (rows_to.at[s, 0], rows_from.at[s, 1]),
            (rows_to.at[s, 1], rows_from.at[s, 0]),
            (pack.at[s], pack_from.at[s, 1]),
            (pack.at[s], pack_from.at[s, 0]),
        )
        copies = []
        for to, (src, dst) in enumerate(pairs):
            copies.append(
                pltpu.make_async_remote_copy(
                    src_ref=src,
                    dst_ref=dst,
                    send_sem=send_h.at[s, to],
                    recv_sem=recv_h.at[s, to],
                    device_id=neighbours[to][1],
                    device_id_type=MESH,
                )
            )
        return copies

    def wait_bytes(ref, sem):
        pltpu.make_async_copy(ref, ref, sem).wait()

    def start_halo(s):
        for (there, _), copy in zip(neighbours, halo_copies(s)):
            pl.when(there)(copy.start)

    def start_a(s):
        @pl.loop(0, n_lat - 1)
        def _(i):
            k = i if s == 0 else jnp.where(edge_a, n_lat - 2 - i, i)
            pltpu.make_async_remote_copy(
                src_ref=gathered.at[s, a, pl.ds(0, comps)],
                dst_ref=gathered.at[s, a, pl.ds(0, comps)],
                send_sem=send_a.at[s],
                recv_sem=recv_a.at[s],
                device_id=(p, lax.rem(a + far_first(k), n_lat), b),
                device_id_type=MESH,
            ).start()

    def help_copy(i):
        return pltpu.make_async_remote_copy(
            src_ref=gathered.at[1, a, pl.ds(0, comps)],
            dst_ref=helped.at[a, pl.ds(0, comps)],
            send_sem=send_x.at[i],
            recv_sem=recv_x,
            device_id=(p, i * (n_lat - 1), twin),
            device_id_type=MESH,
        )

    def wait_a(s, sem):
        wait_bytes(gathered.at[s, pl.ds(0, n_lat - 1), pl.ds(0, comps)], sem.at[s])

    def send_slots():
        def send(start, dst, kind):
            size = dst.shape[-1]

            @pl.loop(0, n_lon)
            def _(k):
                pltpu.make_async_remote_copy(
                    src_ref=slots.at[0, 0, :, pl.ds(start, size)],
                    dst_ref=dst,
                    send_sem=send_i.at[kind],
                    recv_sem=recv_i.at[kind],
                    device_id=(other, a, k),
                    device_id_type=MESH,
                ).start()

        pl.when(first_a)(lambda: send(0, idx_rows.at[b], 0))
        pl.when(last_a)(lambda: send(2 * cols, idx_rows.at[b], 0))
        pl.when(first_b)(lambda: send(4 * cols, idx_sides.at[0], 1))
        pl.when(last_b)(lambda: send(4 * cols + 2 * rows, idx_sides.at[1], 1))

    def wait_slots():
        pl.when(edge_a)(lambda: wait_bytes(idx_rows, recv_i.at[0]))
        wait_bytes(idx_sides, recv_i.at[1])

    groups = -(-n_lat * n_slots // cols)
    lane8 = lane[0:8]

    def settle(block_of, packed):
        for level in range(levels):
            totals = [jnp.zeros((8, cols), jnp.float32)] * groups
            for k in range(n_lat):
                low, high = k * n_slots, (k + 1) * n_slots
                turned = pltpu.roll(block_of[k], (low - level * half) % cols, 1)
                for g in range(low // cols, (high - 1) // cols + 1):
                    here = jnp.logical_and(lane8 >= low - g * cols, lane8 < high - g * cols)
                    totals[g] = jnp.where(here, turned, totals[g])
            for g in range(groups):
                packed[level, g] = totals[g]

    def pick(packed, column, wanted):
        device = ((wanted >> 4) * 21846) >> 16
        row_of = device >> (n_lon.bit_length() - 1)
        number = wanted - (device - row_of) * n_slots
        group = jnp.where(device - row_of * n_lon == column, number >> (cols.bit_length() - 1), -1)
        group = jnp.broadcast_to(group, (8, cols))
        place = jnp.broadcast_to(number & (cols - 1), (8, cols))
        totals = [jnp.zeros((8, cols), jnp.float32)] * levels
        for g in range(groups):
            mine = group == g
            for level in range(levels):
                totals[level] = jnp.where(mine, lane_take(packed[level, g], place), totals[level])
        return totals

    order = row_order(n_lon)
    late = len(order) // 2

    def part_copy(s, src, dst, sem, kind, k):
        return pltpu.make_async_remote_copy(
            src_ref=src,
            dst_ref=dst,
            send_sem=sem,
            recv_sem=recv_b.at[s, kind],
            device_id=(other, a, k),
            device_id_type=MESH,
        )

    def send_rows(s, packed, column, held, sem, first, last):
        @pl.loop(first, last)
        def _(group):
            to_whom = [column ^ pick_at(group, way) for way in zip(*order)]
            for k in to_whom:
                for t in range(2):
                    wanted = idx_rows[k, :, t * cols : (t + 1) * cols]
                    for level, total in enumerate(pick(packed, column, wanted)):
                        held[k, t, level] = total
            for k in to_whom:
                src = held.at[k, :, :, pl.ds(0, comps)]
                dst = row_rim.at[s, column, :, :, pl.ds(0, comps)]
                part_copy(s, src, dst, sem, 0, k).start()

    def send_parts(s):
        settle(gathered.at[s], dense.at[s])
        for side in range(2):
            for level, total in enumerate(pick(dense.at[s], b, idx_sides[side])):
                side_parts[s, side, level] = total
            src = side_parts.at[s, side, :, pl.ds(0, comps)]
            dst = side_rim.at[s, b, :, pl.ds(0, comps)]
            part_copy(s, src, dst, send_b.at[s, 1], 1, side * (n_lon - 1)).start()

        @pl.when(edge_a)
        def _():
            last = len(order) if s == 0 else jnp.where(edge_b, late, len(order))
            send_rows(s, dense.at[s], b, row_parts.at[s], send_b.at[s, 0], 0, last)

    def help_out():
        wait_bytes(helped.at[:, pl.ds(0, comps)], recv_x)
        settle(helped, dense_x)
        send_rows(1, dense_x, twin, row_parts_x, send_y, late, len(order))

    def take_rim(s):
        @pl.when(edge_a)
        def _():
            wait_bytes(row_rim.at[s, :, :, :, pl.ds(0, comps)], recv_b.at[s, 0])
            total = jnp.sum(row_rim[s], axis=0)

            def put(at):
                for t in range(2):
                    for level in range(levels):
                        for c in range(comps):
                            ext[s, c, level, at + t : at + t + 1, :] = total[t, level, c : c + 1, :]

            pl.when(first_a)(lambda: put(PAD - 2))
            pl.when(last_a)(lambda: put(PAD + rows))

        @pl.when(edge_b)
        def _():
            wait_bytes(side_rim.at[s, :, :, pl.ds(0, comps)], recv_b.at[s, 1])
            total = jnp.sum(side_rim[s], axis=0)

            def put(side):
                for level in range(levels):
                    both = (total[level], pltpu.roll(total[level], half, 1))
                    for t in range(2):
                        for c in range(comps):
                            at = 4 * (c * levels + level) + 2 * side + t
                            flip[at : at + 1, :] = both[t][c : c + 1, :]
                pack_from[s, side] = flip[...].T[0:rows, :]

            pl.when(first_b)(lambda: put(0))
            pl.when(last_b)(lambda: put(1))

    def wait_halo(s):
        landed = (rows_from.at[s, 0], rows_from.at[s, 1], pack_from.at[s, 0], pack_from.at[s, 1])
        for side_of, opposite in ((UP, DOWN), (DOWN, UP), (LEFT, RIGHT), (RIGHT, LEFT)):

            @pl.when(neighbours[side_of][0])
            def _():
                wait_bytes(landed[side_of], recv_h.at[s, opposite])
                if side_of in (UP, DOWN):
                    at = PAD - 2 if side_of == UP else PAD + rows
                    for f in range(comps * levels):
                        ext[s, f // levels, f % levels, at : at + 2, :] = rows_from[s, side_of, f]

    def rates(s, emit, low_row=0, count=0):
        chunk = count or rows
        for base in (low_row,):
            lanes = lane[0:chunk]
            beside = jnp.where(
                lanes & 2 == 0,
                pack_from[s, 0, base : base + chunk, :],
                pack_from[s, 1, base : base + chunk, :],
            )

            def at(c, level, shift=0):
                low = PAD + base + shift
                return ext[s, c, level, low : low + chunk, :]

            for level in range(levels):
                u1, u2 = at(1, level) * (1.0 / 12.0), at(2, level) * (1.0 / 12.0)
                b1, b2 = at(4, level) * (1.0 / 12.0), at(5, level) * (1.0 / 12.0)

                def terms(c, with_b):
                    mid = at(c, level)
                    around = pltpu.roll(beside, (cols - 2 - 4 * (c * levels + level)) % cols, 1)
                    west1 = pltpu.roll(jnp.where(lanes == cols - 1, around, mid), 1, 1)
                    west2 = pltpu.roll(jnp.where(lanes >= cols - 2, around, mid), 2, 1)
                    east1 = pltpu.roll(jnp.where(lanes == 0, around, mid), cols - 1, 1)
                    east2 = pltpu.roll(jnp.where(lanes < 2, around, mid), cols - 2, 1)
                    north1, south1 = at(c, level, -1), at(c, level, 1)
                    d_lat = 8.0 * (south1 - north1) - (at(c, level, 2) - at(c, level, -2))
                    d_lon = 8.0 * (east1 - west1) - (east2 - west2)
                    lap = south1 + north1 + east1 + west1 + at(c, 1 - level) - 6.0 * mid
                    adv_u = u1 * d_lat + u2 * d_lon
                    adv_b = b1 * d_lat + b2 * d_lon if with_b else None
                    return mid, adv_u, adv_b, DIFFUSION * lap

                for c in range(3):
                    mid, adv_u, adv_b, lap = terms(c, True)
                    mid_b, adv_ub, adv_bb, lap_b = terms(c + 3, True)
                    moment = adv_bb - adv_u + lap
                    if c == 0:
                        moment = moment + BUOYANCY * at(6, level)
                    emit(c, level, base, mid, moment)
                    emit(c + 3, level, base, mid_b, adv_b - adv_ub + lap_b)
                mid, adv_u, _, lap = terms(6, False)
                emit(6, level, base, mid, lap - adv_u)

    def first_section(c, level, base, mid, rate):
        ext[1, c, level, PAD + base : PAD + base + mid.shape[0], :] = mid + STEP * rate

    def second_section(c, level, base, mid, rate):
        start = ext[0, c, level, PAD + base : PAD + base + mid.shape[0], :]
        out[0, c, level, base : base + mid.shape[0], :] = 0.5 * start + 0.5 * (mid + STEP * rate)

    def give(s):
        donate(s)
        if s == 0:
            pack_sides(s)
            pack_rows(s)
            pl.semaphore_wait(barrier, greeted)
        if s == 1:
            for i in range(2):
                pl.when(edge_b)(help_copy(i).start)
        start_a(s)
        if s == 0:
            send_slots()
        if s == 1:
            pack_sides(s)
            pack_rows(s)
        start_halo(s)

    def mend_side(s):
        rim = jnp.where(first_b, pack_from[s, 0], pack_from[s, 1])
        spot = lane & 3
        near_w, far_w = pltpu.roll(rim, 1, 1), pltpu.roll(rim, 2, 1)
        near_e, far_e = pltpu.roll(rim, cols - 1, 1), pltpu.roll(rim, cols - 2, 1)
        slope = jnp.where(
            spot == 2,
            far_w - 8.0 * near_w,
            jnp.where(spot == 3, far_w, jnp.where(spot == 1, 8.0 * near_e - far_e, -far_e)),
        ) * (1.0 / 12.0)
        lap = jnp.where(spot == 2, near_w, jnp.where(spot == 1, near_e, 0.0))
        per_comp = 4 * levels
        within = lane & (per_comp - 1)
        u2 = lane_take(pack[s], within + 2 * per_comp)
        b2 = lane_take(pack[s], within + 5 * per_comp)
        swap = 3 * per_comp
        partner = jnp.where(
            lane < swap,
            pltpu.roll(slope, cols - swap, 1),
            jnp.where(lane < 2 * swap, pltpu.roll(slope, swap, 1), 0.0),
        )
        scale = STEP if s == 0 else 0.5 * STEP
        change = scale * (DIFFUSION * lap - u2 * slope + b2 * partner)
        outer = jnp.logical_or(lane >= cols - 2, lane < 2)
        for f in range(comps * levels):
            c, level = f // levels, f % levels
            here = jnp.where(outer, pltpu.roll(change, (cols - 2 - 4 * f) % cols, 1), 0.0)
            if s == 0:
                ext[1, c, level, PAD : PAD + rows, :] = inner(1, c, level) + here
            else:
                out[0, c, level] = out[0, c, level] + here

    def mend(s, emit):
        take_rim(s)
        pl.when(edge_b)(lambda: mend_side(s))
        pl.when(first_a)(lambda: rates(s, emit, 0, 8))
        pl.when(last_a)(lambda: rates(s, emit, rows - 8, 8))

    flip[...] = jnp.zeros_like(flip)
    for s in range(2):

        @pl.when(first_b)
        def _():
            pack_from[s, 0] = jnp.zeros((rows, cols), jnp.float32)

        @pl.when(last_b)
        def _():
            pack_from[s, 1] = jnp.zeros((rows, cols), jnp.float32)

    loads[3].wait()
    give(0)
    wait_halo(0)
    rates(0, first_section)
    wait_a(0, recv_a)
    wait_slots()
    send_parts(0)

    pl.when(edge)(lambda: mend(0, first_section))
    give(1)

    wait_a(1, recv_a)
    send_parts(1)
    wait_halo(1)
    rates(1, second_section)
    pl.when(helps)(help_out)
    for s in range(2):
        wait_a(s, send_a)
        for (there, _), copy in zip(neighbours, halo_copies(s)):
            pl.when(there)(copy.wait_send)
    pl.when(edge_a)(lambda: wait_bytes(idx_rows, send_i.at[0]))
    pl.when(edge_b)(lambda: wait_bytes(idx_rows.at[pl.ds(0, n_lon // 2)], send_i.at[1]))

    pl.when(edge)(lambda: mend(1, second_section))

    for s in range(2):
        wait_bytes(side_parts.at[s, :, :, pl.ds(0, comps)], send_b.at[s, 1])
    shared = n_lon * late // len(order)
    sent = [row_parts.at[s, :, :, :, pl.ds(0, comps)] for s in range(2)]
    half_sent = row_parts.at[1, pl.ds(0, shared), :, :, pl.ds(0, comps)]
    rest_sent = row_parts_x.at[pl.ds(0, n_lon - shared), :, :, pl.ds(0, comps)]
    pl.when(edge_a)(lambda: wait_bytes(sent[0], send_b.at[0, 0]))
    inside = jnp.logical_and(edge_a, jnp.logical_not(edge_b))
    pl.when(inside)(lambda: wait_bytes(sent[1], send_b.at[1, 0]))
    pl.when(jnp.logical_and(edge_a, edge_b))(lambda: wait_bytes(half_sent, send_b.at[1, 0]))
    pl.when(helps)(lambda: wait_bytes(rest_sent, send_y))
    for i in range(2):
        pl.when(edge_b)(help_copy(i).wait_send)


def solution(mesh):
    n_lat, n_lon = mesh.shape["lat"], mesh.shape["lon"]

    def per_device(state, source_slot, donor_cell, donor_frac, donor_turn):
        _, comps, levels, rows, cols = state.shape
        f32, i32, dma = jnp.float32, jnp.int32, pltpu.SemaphoreType.DMA
        vmem = pl.BlockSpec(memory_space=pltpu.VMEM)
        return pl.pallas_call(
            functools.partial(kernel, n_lat, n_lon),
            out_shape=jax.ShapeDtypeStruct(state.shape, f32),
            in_specs=[pl.BlockSpec(memory_space=pltpu.HBM)] * 5,
            out_specs=vmem,
            scratch_shapes=[
                pltpu.VMEM((2, comps, levels, rows + 2 * PAD, cols), f32),
                pltpu.VMEM((1, donor_cell.shape[3]), i32),
                pltpu.VMEM((1, donor_cell.shape[3]), f32),
                pltpu.VMEM((2, donor_cell.shape[3]), f32),
                pltpu.VMEM((8, cols), i32),
                pltpu.VMEM((8, cols), f32),
                pltpu.VMEM((2, 2, comps * levels, 2, cols), f32),
                pltpu.VMEM((2, 2, comps * levels, 2, cols), f32),
                pltpu.VMEM((2, rows, cols), f32),
                pltpu.VMEM((2, 2, rows, cols), f32),
                pltpu.VMEM((2, n_lat, 8, cols), f32),
                pltpu.VMEM((2, levels, -(-n_lat * donor_cell.shape[3] // cols), 8, cols), f32),
                pltpu.VMEM((n_lon, 1, 2 * cols), i32),
                pltpu.VMEM((2, 1, 2 * rows), i32),
                pltpu.VMEM((2, n_lon, 2, levels, 8, cols), f32),
                pltpu.VMEM((2, 2, levels, 8, cols), f32),
                pltpu.VMEM((2, n_lon, 2, levels, 8, cols), f32),
                pltpu.VMEM((2, n_lon, levels, 8, cols), f32),
                pltpu.VMEM((cols, cols), f32),
                pltpu.VMEM((n_lat, 8, cols), f32),
                pltpu.VMEM((levels, -(-n_lat * donor_cell.shape[3] // cols), 8, cols), f32),
                pltpu.VMEM((n_lon, 2, levels, 8, cols), f32),
                dma((4,)),
                dma((2,)),
                dma((2,)),
                dma((2, 4)),
                dma((2, 4)),
                dma((2,)),
                dma((2,)),
                dma((2, 2)),
                dma((2, 2)),
                dma((2,)),
                dma,
                dma,
            ],
            compiler_params=pltpu.CompilerParams(
                collective_id=0, has_side_effects=True, vmem_limit_bytes=32 * 2**20
            ),
        )(
            *(
                pltpu.with_memory_space_constraint(x, pltpu.HBM)
                for x in (state, source_slot, donor_cell, donor_frac, donor_turn)
            )
        )

    in_specs = (
        P("panel", None, None, "lat", "lon"),
        P("panel", "lat", "lon", None),
        P("panel", "lat", "lon", None),
        P("panel", "lat", "lon", None, None),
        P("panel", "lat", "lon", None),
    )
    out_specs = P("panel", None, None, "lat", "lon")
    return jax.shard_map(
        per_device, mesh=mesh, in_specs=in_specs, out_specs=out_specs, check_vma=False
    )
```
